256 devices in a mesh: wide: 64 (over y, z_hi, x), narrow: 4 (over z_lo, core).
Axes of the slice: x: 4, y: 4, z: 8 (z_hi: 4, z_lo: 2; z = z_hi * 2 + z_lo), core: 2. Of those that a mesh axis runs over, the one named last changes fastest.
Arguments:
- sources: bfloat16 [524288, 512], P(('wide', 'narrow')), may hold values from -6 to 6
- order: int32 [524288], P(('wide', 'narrow')), may hold values from 0 to 524287, as said below
- near_cols: int32 [4096, 8], P(('wide', 'narrow')), may hold values from 0 to 4095, as said below
- near_blocks: bfloat16 [4096, 8, 128, 128], P(('wide', 'narrow')), may hold values from -0.1875 to 0.1875
- in_basis: bfloat16 [524288, 256], P(('wide', 'narrow')), may hold values from -0.0625 to 0.0625
- transfer: bfloat16 [4, 64, 2, 256, 256], P(None, 'wide'), may hold values from -0.25 to 0.25
- out_basis: bfloat16 [524288, 256], P(('wide', 'narrow')), may hold values from -0.375 to 0.375
Outputs:
- potential: bfloat16 [524288, 512], P(('wide', 'narrow'))
The draws below stay inside these ranges and needn't reach their ends.
Inputs may be any that keep to these rules, and one draw needn't show every extreme that they name: order maps each aligned run of 2048 rows onto itself, each row once. `near_cols`: each row block r lists distinct offsets from -4 to 4; the id is r plus the offset, clamped into r's cluster of 64 blocks.
All inputs are finite; a program needn't handle non-finite values.
Results may differ from the reference program's by a relative error of at most 0.014.
Values may be sent and summed in bfloat16 or wider, within the bound.
A program may use at most 128 MiB of HBM per device.

```python
import jax
import jax.numpy as jnp
from jax import lax

RANK = 256
BLOCK = 128
RHS = 512
ROWS_DEV = 2048
LEVELS = 4
REACH = 4
NEAR = 8
N_ROWS = 524288
BLOCKS = 4096
CLUSTER_ROWS = 8192
N_WIDE = 64
N_NARROW = 4


def draw_order(key, part):
    key = jax.random.fold_in(key, 1)
    devices = N_WIDE * N_NARROW
    keys = jax.random.split(key, devices)
    perms = jax.vmap(lambda one: jax.random.permutation(one, ROWS_DEV))(keys).astype(jnp.int32)
    offsets = (jnp.arange(devices, dtype=jnp.int32) * ROWS_DEV)[:, None]
    return (perms + offsets).reshape(-1).astype(jnp.int32)


def draw_near_cols(key, part):
    key = jax.random.fold_in(key, 2)
    total = N_WIDE * N_NARROW * ROWS_DEV // BLOCK
    cblocks = ROWS_DEV * N_NARROW // BLOCK
    keys = jax.random.split(key, total)
    perms = jax.vmap(lambda one: jax.random.permutation(one, 2 * REACH + 1))(keys).astype(jnp.int32)
    shifts = perms[:, :NEAR] - REACH
    rowids = jnp.arange(total, dtype=jnp.int32)[:, None]
    lower = rowids // cblocks * cblocks
    return jnp.clip(rowids + shifts, lower, lower + cblocks - 1).astype(jnp.int32)


def block_levels(stream_key, shape, cuts, low, high):
    gain, own = 1.0, jax.random.fold_in(stream_key, 6)
    for dim, shards_of in cuts:
        heights = jnp.exp(jax.random.uniform(jax.random.fold_in(own, dim), (shards_of,), jnp.float32, low / len(cuts), high / len(cuts)))
        gain = gain * jnp.repeat(heights, shape[dim] // shards_of).reshape([-1 if axis == dim else 1 for axis in range(len(shape))])
    return gain


def normal_values(key, dims, deviation, most, cuts=(), held_as=jnp.bfloat16):
    drawn = deviation * jax.random.normal(key, dims, jnp.float32)
    if cuts:
        drawn = drawn * block_levels(key, dims, cuts, -0.22, 0.18)
    return jnp.clip(drawn, -most, most).astype(held_as)


def setup_inputs(seed: int = 0) -> dict:
    splits = jax.random.split(jax.random.key(seed), 8)
    return {
        "sources": normal_values(splits[0], (N_ROWS, RHS), 1.0, 6.0, ((0, 256),)),
        "order": draw_order(jax.random.fold_in(splits[7], 71), 0),
        "near_cols": draw_near_cols(jax.random.fold_in(splits[7], 71), 0),
        "near_blocks": normal_values(splits[3], (BLOCKS, NEAR, BLOCK, BLOCK), (BLOCK * NEAR) ** -0.5, 0.1875, ((0, 256),)),
        "in_basis": normal_values(splits[4], (N_ROWS, RANK), CLUSTER_ROWS ** -0.5, 0.0625, ((0, 256),)),
        "transfer": normal_values(splits[5], (LEVELS, N_WIDE, 2, RANK, RANK), (2 * RANK) ** -0.5, 0.25, ((1, 64),)),
        "out_basis": normal_values(splits[6], (N_ROWS, RANK), RANK ** -0.5, 0.375, ((0, 256),)),
    }


def reference(sources, order, near_cols, near_blocks, in_basis, transfer, out_basis):
    clusters = N_WIDE
    crows = ROWS_DEV * N_NARROW
    cblocks = crows // BLOCK
    permuted = jnp.take(sources, order, axis=0)
    xcl = permuted.reshape(clusters, crows, RHS)
    vcl = in_basis.reshape(clusters, crows, RANK)
    ucl = out_basis.reshape(clusters, crows, RANK)

    def project(pair):
        return jnp.dot(pair[0].T, pair[1], preferred_element_type=jnp.float32)

    coeff = lax.map(project, (vcl, xcl)).astype(jnp.bfloat16)
    bits = int(N_WIDE).bit_length() - 1
    ident = jnp.arange(clusters, dtype=jnp.int32)
    for level in range(LEVELS):
        partner_ids = jnp.bitwise_xor(ident, jnp.int32(1 << (level % bits)))
        partner = jnp.take(coeff, partner_ids, axis=0)
        blocks = transfer[level].astype(jnp.float32)
        summed = (jnp.einsum('wij,wjc->wic', blocks[:, 0], coeff.astype(jnp.float32))
                  + jnp.einsum('wij,wjc->wic', blocks[:, 1], partner.astype(jnp.float32)))
        coeff = summed.astype(jnp.bfloat16)
    coarse = coeff
    cols_cl = near_cols.reshape(clusters, cblocks, NEAR)
    kcl = near_blocks.reshape(clusters, cblocks, NEAR, BLOCK, BLOCK)

    def one_cluster(items):
        xrows, ubase, ccoef, cols, kblocks, which = items
        far = jnp.dot(ubase, ccoef, preferred_element_type=jnp.float32)
        xblocks = xrows.reshape(cblocks, BLOCK, RHS)
        local_ids = (cols - which * cblocks).astype(jnp.int32)
        picked = jnp.take(xblocks, local_ids, axis=0)
        near = jnp.einsum('reij,rejc->ric', kblocks.astype(jnp.float32), picked.astype(jnp.float32))
        return (far + near.reshape(crows, RHS)).astype(jnp.bfloat16)

    result = lax.map(one_cluster, (xcl, ucl, coarse, cols_cl, kcl, ident))
    return result.reshape(N_ROWS, RHS)
```

```python
import functools

import jax
import jax.numpy as jnp
from jax import lax
from jax.experimental import pallas as pl
from jax.experimental.pallas import tpu as pltpu
from jax.sharding import PartitionSpec as P

F32, BF16, I32 = jnp.float32, jnp.bfloat16, jnp.int32
MESH = pl.DeviceIdType.MESH
ROWS = 2048
RHS = 512
RANK = 256
BLOCK = 128
REACH = 4
NEAR = 8
BLOCKS_DEV = ROWS // BLOCK
OFFSETS = 2 * REACH + 1
CLUSTER_BLOCKS = 64
HALO = REACH * BLOCK
QUARTER = RHS // 4
GATHER_ROWS = 512
SCATTER_ROWS = 1024
VMEM, SMEM, DMA = pltpu.VMEM, pltpu.SMEM, pltpu.SemaphoreType.DMA


def flip(index, bit):
    return index + bit - 2 * bit * ((index // bit) % 2)


def dot(a, b):
    return jnp.dot(a, b, preferred_element_type=F32)


def tree_kernel(
    order_h, cols_h, sources_h, basis_h, blocks_h, transfer_h,
    coarse_o, near_o,
    order, cols, sources, basis, blocks, transfer,
    order_col, table_v, table_s, moved, permuted, part, part_b, core_in,
    z_out, z_in, c0, x_in, transfer_x, c2, h1_in, c3, h2_in, coarse,
    load, table_sem, send, recv, halo_send, halo_recv,
):
    w, n = lax.axis_index("wide"), lax.axis_index("narrow")
    first_row = (w * 4 + n) * ROWS
    quarter = flip(n, 2) * ((w // 8) % 2) + n * (1 - (w // 8) % 2)
    core = (w, flip(n, 1))
    zside = (w, flip(n, 2))
    cross = (w, flip(flip(n, 1), 2))
    x1, x2, x3 = (flip(w, 1), n), (flip(w, 2), n), (flip(flip(w, 1), 2), n)
    h1, h2 = (flip(w, 4), n), (flip(w, 8), flip(n, 2))

    loads = [
        pltpu.make_async_copy(a, b, load.at[i])
        for i, (a, b) in enumerate(
            (
                (order_h, order),
                (basis_h, basis),
                (sources_h, sources),
                (cols_h, cols),
                (transfer_h, transfer),
                (blocks_h, blocks),
            )
        )
    ]
    for one in loads:
        one.start()
    barrier = pltpu.get_barrier_semaphore()
    partners = (core, zside, cross, x1, x2, x3, h1, h2)
    for who in partners:
        pl.semaphore_signal(barrier, inc=1, device_id=who, device_id_type=MESH)

    def remote(src, dst, i, who):
        return pltpu.make_async_remote_copy(
            src_ref=src, dst_ref=dst, send_sem=send.at[i], recv_sem=recv.at[i],
            device_id=who, device_id_type=MESH,
        )

    loads[0].wait()
    loads[1].wait()

    def move(b, _):
        at = pl.multiple_of(b * SCATTER_ROWS, SCATTER_ROWS)
        ids = lax.broadcasted_iota(I32, (SCATTER_ROWS, BLOCK), 0) + (first_row + at)
        hot = jnp.concatenate(
            [jnp.where(ids == order[k : k + 1, :], 1.0, 0.0).astype(BF16) for k in range(BLOCKS_DEV)],
            axis=1,
        )
        moved[pl.ds(at, SCATTER_ROWS), :] = dot(hot, basis[...]).astype(BF16)
        return 0

    lax.fori_loop(0, ROWS // SCATTER_ROWS, move, 0)
    loads[4].wait()
    pl.semaphore_wait(barrier, len(partners))
    send_tx = remote(transfer.at[0], transfer_x, 0, x2)
    send_tx.start()

    loads[2].wait()
    term = lax.dot_general(
        moved[...], sources[...], (((0,), (0,)), ((), ())), preferred_element_type=F32
    )
    for k in range(4):
        piece = term[:, k * QUARTER : (k + 1) * QUARTER]
        part[k] = piece
        part_b[k] = piece.astype(BF16)
    q1, q2 = flip(quarter, 1), flip(quarter, 2)
    q3 = flip(q1, 2)
    send_c1 = remote(part_b.at[q3], core_in.at[1], 1, core)
    send_c0 = remote(part_b.at[q1], core_in.at[0], 2, core)
    send_c1.start()
    send_c0.start()

    turned = order[...].T
    for k in range(BLOCKS_DEV):
        order_col[k] = jnp.broadcast_to(turned[:, k : k + 1], (BLOCK, BLOCK))

    def gather(b, _):
        lanes = lax.broadcasted_iota(I32, (BLOCK, BLOCK), 1) + first_row
        rows = []
        for k in range(GATHER_ROWS // BLOCK):
            ids = order_col[b * (GATHER_ROWS // BLOCK) + k]
            rows.append(
                jnp.concatenate(
                    [jnp.where(lanes + c * BLOCK == ids, 1.0, 0.0).astype(BF16) for c in range(BLOCKS_DEV)],
                    axis=1,
                )
            )
        hot = jnp.concatenate(rows, axis=0)
        at = pl.multiple_of(b * GATHER_ROWS + HALO, HALO)
        permuted[pl.ds(at, GATHER_ROWS), :] = dot(hot, sources[...]).astype(BF16)
        return 0

    gather(3, 0)

    send_c1.wait_recv()
    z_out[...] = (part[q2] + core_in[1].astype(F32)).astype(BF16)
    send_z = remote(z_out, z_in, 3, zside)
    send_z.start()

    loads[3].wait()
    listed = cols[...]
    lane = lax.broadcasted_iota(I32, (NEAR, BLOCKS_DEV), 1)
    entry = lax.broadcasted_iota(I32, (NEAR, BLOCKS_DEV), 0)
    rank = jnp.zeros((NEAR, BLOCKS_DEV), I32)
    for e in range(NEAR - 1):
        same = jnp.where(listed == listed[e : e + 1, :], 1, 0)
        rank = rank + jnp.where(entry > e, same, 0)
    slot = listed - lane - (w * 4 + n) * BLOCKS_DEV + REACH
    slot = slot + jnp.where(listed == w * CLUSTER_BLOCKS, -rank, rank)
    for d in range(OFFSETS):
        table_v[d : d + 1, :BLOCKS_DEV] = jnp.sum(
            jnp.where(slot == d, entry + 1, 0), axis=0, keepdims=True
        )
    table_copy = pltpu.make_async_copy(table_v, table_s, table_sem)
    table_copy.start()

    gather(0, 0)

    send_c0.wait_recv()
    own = part[quarter] + core_in[0].astype(F32)
    send_z.wait_recv()
    c0[...] = (own + z_in[...].astype(F32)).astype(BF16)
    send_x = [remote(c0, x_in.at[i], 4 + i, who) for i, who in enumerate((x1, x2, x3))]
    for one in send_x:
        one.start()

    def halo_copy(up):
        if up:
            src, dst, who = permuted.at[pl.ds(ROWS, HALO)], permuted.at[pl.ds(0, HALO)], (n + 1) % 4
        else:
            src, dst, who = permuted.at[pl.ds(HALO, HALO)], permuted.at[pl.ds(ROWS + HALO, HALO)], (n + 3) % 4
        return pltpu.make_async_remote_copy(
            src_ref=src, dst_ref=dst, send_sem=halo_send.at[up], recv_sem=halo_recv.at[up],
            device_id=(w, who), device_id_type=MESH,
        )

    @pl.when(n < 3)
    def _():
        halo_copy(1).start()

    @pl.when(n > 0)
    def _():
        halo_copy(0).start()

    @pl.when(n == 0)
    def _():
        for k in range(REACH):
            permuted[k * BLOCK : (k + 1) * BLOCK, :] = permuted[HALO : HALO + BLOCK, :]

    @pl.when(n == 3)
    def _():
        for k in range(REACH):
            at = ROWS + HALO + k * BLOCK
            permuted[at : at + BLOCK, :] = permuted[ROWS + HALO - BLOCK : ROWS + HALO, :]

    lax.fori_loop(1, 3, gather, 0)
    table_copy.wait()
    loads[5].wait()

    def near_pair(p, _):
        def row(r):
            found = []
            for d in range(OFFSETS):
                at = table_s[d, r]
                block = blocks[r, jnp.maximum(at - 1, 0)]
                found.append(jnp.where(at > 0, block, jnp.zeros_like(block)))
            return found

        none = jnp.zeros((BLOCK, BLOCK), BF16)
        upper = jnp.concatenate(row(2 * p) + [none], axis=1)
        lower = jnp.concatenate([none] + row(2 * p + 1), axis=1)
        at = pl.multiple_of(p * 2 * BLOCK, 2 * BLOCK)
        near_o[pl.ds(at, 2 * BLOCK), :] = dot(
            jnp.concatenate([upper, lower], axis=0),
            permuted[pl.ds(at, (OFFSETS + 1) * BLOCK), :],
        )
        return 0

    lax.fori_loop(2, 5, near_pair, 0)

    for one in send_x:
        one.wait_recv()
    send_tx.wait_recv()
    c1 = (dot(transfer[0, 0], c0[...]) + dot(transfer[0, 1], x_in[0])).astype(BF16)
    c1x = (dot(transfer_x[0], x_in[1]) + dot(transfer_x[1], x_in[2])).astype(BF16)
    c2[...] = (dot(transfer[1, 0], c1) + dot(transfer[1, 1], c1x)).astype(BF16)
    send_h1 = remote(c2, h1_in, 7, h1)
    send_h1.start()

    lax.fori_loop(5, 6, near_pair, 0)

    @pl.when(n > 0)
    def _():
        halo_copy(1).wait_recv()

    @pl.when(n < 3)
    def _():
        halo_copy(0).wait_recv()

    lax.fori_loop(0, 2, near_pair, 0)

    send_h1.wait_recv()
    c3[...] = (dot(transfer[2, 0], c2[...]) + dot(transfer[2, 1], h1_in[...])).astype(BF16)
    send_h2 = remote(c3, h2_in, 8, h2)
    send_h2.start()

    lax.fori_loop(6, 8, near_pair, 0)

    send_h2.wait_recv()
    coarse[quarter] = (dot(transfer[3, 0], c3[...]) + dot(transfer[3, 1], h2_in[...])).astype(BF16)
    send_a = remote(coarse.at[quarter], coarse.at[quarter], 9, zside)
    send_b = remote(coarse.at[quarter], coarse.at[quarter], 10, core)
    send_a.start()
    send_b.start()
    remote(coarse.at[q2], coarse.at[q2], 9, zside).wait_recv()
    send_f = remote(coarse.at[q2], coarse.at[q2], 11, core)
    send_f.start()

    send_tx.wait_send()
    for one in (send_c0, send_c1, send_z, *send_x, send_h1, send_h2, send_a, send_b):
        one.wait_send()

    @pl.when(n < 3)
    def _():
        halo_copy(1).wait_send()

    @pl.when(n > 0)
    def _():
        halo_copy(0).wait_send()

    send_f.wait_send()
    remote(coarse.at[q1], coarse.at[q1], 10, core).wait_recv()
    remote(coarse.at[q3], coarse.at[q3], 11, core).wait_recv()
    coarse_o[...] = coarse[...]


def tree(order, cols, sources, basis, blocks, transfer):
    quarter = (RANK, QUARTER)
    scratch = [
        VMEM((BLOCKS_DEV, BLOCK), I32),
        VMEM((NEAR, BLOCKS_DEV), I32),
        VMEM((ROWS, RHS), BF16),
        VMEM((ROWS, RANK), BF16),
        VMEM((BLOCKS_DEV, NEAR, BLOCK, BLOCK), BF16),
        VMEM((4, 2, RANK, RANK), BF16),
        VMEM((BLOCKS_DEV, BLOCK, BLOCK), I32),
        VMEM((16, 128), I32),
        SMEM((16, 128), I32),
        VMEM((ROWS, RANK), BF16),
        VMEM((ROWS + 2 * HALO, RHS), BF16),
        VMEM((4, *quarter), F32),
        VMEM((4, *quarter), BF16),
        VMEM((2, *quarter), BF16),
        VMEM(quarter, BF16),
        VMEM(quarter, BF16),
        VMEM(quarter, BF16),
        VMEM((3, *quarter), BF16),
        VMEM((2, RANK, RANK), BF16),
        VMEM(quarter, BF16),
        VMEM(quarter, BF16),
        VMEM(quarter, BF16),
        VMEM(quarter, BF16),
        VMEM((4, *quarter), BF16),
        DMA((6,)),
        DMA,
        DMA((12,)),
        DMA((12,)),
        DMA((2,)),
        DMA((2,)),
    ]
    return pl.pallas_call(
        tree_kernel,
        out_shape=(VMEM((4, *quarter), BF16), VMEM((ROWS, RHS), F32)),
        in_specs=[pl.BlockSpec(memory_space=pltpu.HBM)] * 6,
        out_specs=[pl.BlockSpec(memory_space=VMEM)] * 2,
        scratch_shapes=scratch,
        compiler_params=pltpu.CompilerParams(
            collective_id=0, has_side_effects=True, vmem_limit_bytes=44 << 20
        ),
        name="tree",
    )(order, cols, sources, basis, blocks, transfer)


OUT_ROWS = 256


def far_kernel(basis_h, coarse, near, out_h, basis, out, load, store):
    count = ROWS // OUT_ROWS

    def rows(ref, i):
        return ref.at[pl.ds(i * OUT_ROWS, OUT_ROWS)]

    loads = [pltpu.make_async_copy(rows(basis_h, i), rows(basis, i), load.at[i]) for i in range(count)]
    stores = [pltpu.make_async_copy(rows(out, i), rows(out_h, i), store.at[i]) for i in range(count)]
    for one in loads:
        one.start()
    whole = jnp.concatenate([coarse[k] for k in range(4)], axis=1)
    for i in range(count):
        loads[i].wait()
        at = pl.ds(i * OUT_ROWS, OUT_ROWS)
        out[at, :] = (dot(basis[at, :], whole) + near[at, :]).astype(BF16)
        stores[i].start()
    for one in stores:
        one.wait()


def far(basis, coarse, near):
    count = ROWS // OUT_ROWS
    return pl.pallas_call(
        far_kernel,
        out_shape=jax.ShapeDtypeStruct((ROWS, RHS), BF16),
        in_specs=[
            pl.BlockSpec(memory_space=pl.ANY),
            pl.BlockSpec(memory_space=VMEM),
            pl.BlockSpec(memory_space=VMEM),
        ],
        out_specs=pl.BlockSpec(memory_space=pl.ANY),
        scratch_shapes=[
            VMEM((ROWS, RANK), BF16),
            VMEM((ROWS, RHS), BF16),
            DMA((count,)),
            DMA((count,)),
        ],
        compiler_params=pltpu.CompilerParams(vmem_limit_bytes=12 << 20),
        name="far",
    )(basis, coarse, near)


def on_device(sources, order, near_cols, near_blocks, in_basis, transfer, out_basis):
    given = (
        order.reshape(BLOCKS_DEV, BLOCK), near_cols.T, sources, in_basis, near_blocks, transfer[:, 0],
    )
    coarse, near = tree(*(pltpu.with_memory_space_constraint(x, pltpu.HBM) for x in given))
    return far(out_basis, coarse, near)


def solution(mesh):
    return jax.shard_map(
        on_device,
        mesh=mesh,
        in_specs=(
            P(("wide", "narrow"), None),
            P(("wide", "narrow")),
            P(("wide", "narrow"), None),
            P(("wide", "narrow"), None, None, None),
            P(("wide", "narrow"), None),
            P(None, "wide", None, None, None),
            P(("wide", "narrow"), None),
        ),
        out_specs=P(("wide", "narrow"), None),
        check_vma=False,
    )
```

```python
import functools

import jax
import jax.numpy as jnp
from jax import lax
from jax.experimental import pallas as pl
from jax.experimental.pallas import tpu as pltpu
from jax.sharding import PartitionSpec as P

F32, BF16, I32 = jnp.float32, jnp.bfloat16, jnp.int32
MESH = pl.DeviceIdType.MESH
ROWS = 2048
RHS = 512
RANK = 256
BLOCK = 128
REACH = 4
NEAR = 8
BLOCKS_DEV = ROWS // BLOCK
OFFSETS = 2 * REACH + 1
CLUSTER_BLOCKS = 64
HALO = REACH * BLOCK
QUARTER = RHS // 4
HALF = RHS // 2
PIECES = 2
PIECE = QUARTER // PIECES
GATHER_ROWS = 512
OUT_ROWS = 512
SCATTER_ROWS = 1024
VMEM, SMEM, DMA = pltpu.VMEM, pltpu.SMEM, pltpu.SemaphoreType.DMA


def flip(index, bit):
    return index + bit - 2 * bit * ((index // bit) % 2)


def dot(a, b):
    return jnp.dot(a, b, preferred_element_type=F32)


def dot_t(a, b):
    return lax.dot_general(a, b, (((1,), (1,)), ((), ())), preferred_element_type=F32)


def piece(p):
    return pl.ds(p * PIECE, PIECE)


def tree_kernel(
    order_h, cols_h, sources_h, basis_h, blocks_h, transfer_h, out_basis_h,
    other_o, near_o, own_o,
    order, cols, sources, basis, blocks, transfer, out_basis,
    order_col, table_v, table_s, moved, permuted, part, part_b, part_in,
    c0, x_in, transfer_x, c2, h1_in, c3, h2_in, coarse,
    load, table_sem, send, recv, halo_send, halo_recv,
):
    w, n = lax.axis_index("wide"), lax.axis_index("narrow")
    first_row = (w * 4 + n) * ROWS
    quarter = flip(n, 2) * ((w // 8) % 2) + n * (1 - (w // 8) % 2)
    core = (w, flip(n, 1))
    zside = (w, flip(n, 2))
    cross = (w, flip(flip(n, 1), 2))
    x1, x2, x3 = (flip(w, 1), n), (flip(w, 2), n), (flip(flip(w, 1), 2), n)
    h1, h2 = (flip(w, 4), n), (flip(w, 8), flip(n, 2))

    loads = [
        pltpu.make_async_copy(a, b, load.at[i])
        for i, (a, b) in enumerate(
            (
                (order_h, order),
                (basis_h, basis),
                (sources_h, sources),
                (transfer_h, transfer),
                (cols_h, cols),
                (blocks_h, blocks),
                (out_basis_h, out_basis),
            )
        )
    ]
    for one in loads[:2]:
        one.start()
    barrier = pltpu.get_barrier_semaphore()
    partners = (core, zside, cross, x1, x2, x3, h1, h2)
    for who in partners:
        pl.semaphore_signal(barrier, inc=1, device_id=who, device_id_type=MESH)

    def remote(src, dst, i, p, who):
        return pltpu.make_async_remote_copy(
            src_ref=src, dst_ref=dst, send_sem=send.at[i, p], recv_sem=recv.at[i, p],
            device_id=who, device_id_type=MESH,
        )

    loads[0].wait()
    loads[2].start()
    loads[1].wait()
    for one in loads[3:]:
        one.start()

    def move(b, _):
        at = pl.multiple_of(b * SCATTER_ROWS, SCATTER_ROWS)
        ids = lax.broadcasted_iota(I32, (SCATTER_ROWS, BLOCK), 0) + (first_row + at)
        hot = jnp.concatenate(
            [jnp.where(ids == order[k : k + 1, :], 1.0, 0.0).astype(BF16) for k in range(BLOCKS_DEV)],
            axis=1,
        )
        moved[pl.ds(at, SCATTER_ROWS), :] = dot(hot, basis[...]).astype(BF16)
        return 0

    lax.fori_loop(0, ROWS // SCATTER_ROWS, move, 0)
    loads[3].wait()
    pl.semaphore_wait(barrier, len(partners))
    side = n % 2
    send_tx = remote(transfer.at[0, side], transfer_x.at[side], 0, 0, x2)
    send_tx.start()

    loads[2].wait()
    half = quarter // 2
    q1, q2 = flip(quarter, 1), flip(quarter, 2)
    q3 = flip(q1, 2)

    def half_term(which):
        columns = sources[:, pl.ds(pl.multiple_of(which * HALF, HALF), HALF)]
        return lax.dot_general(
            columns, moved[...], (((0,), (0,)), ((), ())), preferred_element_type=F32
        )

    pair = (2, QUARTER, RANK)
    part_b[pl.ds(2 - 2 * half, 2)] = half_term(1 - half).astype(BF16).reshape(pair)
    send_c = [
        [
            remote(part_b.at[k, piece(p)], part_in.at[i, piece(p)], 1 + i, p, who)
            for i, (k, who) in enumerate(((q2, zside), (q3, cross), (q1, core)))
        ]
        for p in range(PIECES)
    ]
    for p in range(PIECES):
        for one in send_c[p][:2]:
            one.start()
    term = half_term(half).reshape(pair)
    part[...] = term
    part_b[pl.ds(2 * half, 2)] = term.astype(BF16)
    for p in range(PIECES):
        send_c[p][2].start()

    turned = order[...].T
    for k in range(BLOCKS_DEV):
        order_col[k] = jnp.broadcast_to(turned[:, k : k + 1], (BLOCK, BLOCK))

    def gather(b, _):
        lanes = lax.broadcasted_iota(I32, (BLOCK, BLOCK), 1) + first_row
        rows = []
        for k in range(GATHER_ROWS // BLOCK):
            ids = order_col[b * (GATHER_ROWS // BLOCK) + k]
            rows.append(
                jnp.concatenate(
                    [jnp.where(lanes + c * BLOCK == ids, 1.0, 0.0).astype(BF16) for c in range(BLOCKS_DEV)],
                    axis=1,
                )
            )
        hot = jnp.concatenate(rows, axis=0)
        at = pl.multiple_of(b * GATHER_ROWS + HALO, HALO)
        permuted[pl.ds(at, GATHER_ROWS), :] = dot(hot, sources[...]).astype(BF16)
        return 0

    gather(3, 0)

    loads[4].wait()
    listed = cols[...]
    lane = lax.broadcasted_iota(I32, (NEAR, BLOCKS_DEV), 1)
    entry = lax.broadcasted_iota(I32, (NEAR, BLOCKS_DEV), 0)
    rank = jnp.zeros((NEAR, BLOCKS_DEV), I32)
    for e in range(NEAR - 1):
        same = jnp.where(listed == listed[e : e + 1, :], 1, 0)
        rank = rank + jnp.where(entry > e, same, 0)
    slot = listed - lane - (w * 4 + n) * BLOCKS_DEV + REACH
    slot = slot + jnp.where(listed == w * CLUSTER_BLOCKS, -rank, rank)
    for d in range(OFFSETS):
        table_v[d : d + 1, :BLOCKS_DEV] = jnp.sum(
            jnp.where(slot == d, entry + 1, 0), axis=0, keepdims=True
        )
    table_copy = pltpu.make_async_copy(table_v, table_s, table_sem)
    table_copy.start()

    gather(0, 0)

    send_x = []
    for p in range(PIECES):
        for one in send_c[p]:
            one.wait_recv()
        own = part[quarter % 2, piece(p), :]
        for i in range(3):
            own = own + part_in[i, piece(p), :].astype(F32)
        c0[piece(p), :] = own.astype(BF16)
        send_x.append(
            [
                remote(c0.at[piece(p)], x_in.at[i, piece(p)], 4 + i, p, who)
                for i, who in ((1, x2), (0, x1), (2, x3))
            ]
        )
        for one in send_x[p]:
            one.start()

    def halo_copy(up):
        if up:
            src, dst, who = permuted.at[pl.ds(ROWS, HALO)], permuted.at[pl.ds(0, HALO)], (n + 1) % 4
        else:
            src, dst, who = permuted.at[pl.ds(HALO, HALO)], permuted.at[pl.ds(ROWS + HALO, HALO)], (n + 3) % 4
        return pltpu.make_async_remote_copy(
            src_ref=src, dst_ref=dst, send_sem=halo_send.at[up], recv_sem=halo_recv.at[up],
            device_id=(w, who), device_id_type=MESH,
        )

    @pl.when(n < 3)
    def _():
        halo_copy(1).start()

    @pl.when(n > 0)
    def _():
        halo_copy(0).start()

    @pl.when(n == 0)
    def _():
        for k in range(REACH):
            permuted[k * BLOCK : (k + 1) * BLOCK, :] = permuted[HALO : HALO + BLOCK, :]

    @pl.when(n == 3)
    def _():
        for k in range(REACH):
            at = ROWS + HALO + k * BLOCK
            permuted[at : at + BLOCK, :] = permuted[ROWS + HALO - BLOCK : ROWS + HALO, :]

    gather(1, 0)
    send_tx.wait_recv()
    pass_tx = remote(transfer_x.at[side], transfer_x.at[side], 0, 1, core)
    pass_tx.start()
    gather(2, 0)
    table_copy.wait()
    loads[5].wait()

    def near_pair(p, _):
        def row(r):
            found = []
            for d in range(OFFSETS):
                at = table_s[d, r]
                block = blocks[r, jnp.maximum(at - 1, 0)]
                found.append(jnp.where(at > 0, block, jnp.zeros_like(block)))
            return found

        none = jnp.zeros((BLOCK, BLOCK), BF16)
        upper = jnp.concatenate(row(2 * p) + [none], axis=1)
        lower = jnp.concatenate([none] + row(2 * p + 1), axis=1)
        at = pl.multiple_of(p * 2 * BLOCK, 2 * BLOCK)
        found = dot(
            jnp.concatenate([upper, lower], axis=0),
            permuted[pl.ds(at, (OFFSETS + 1) * BLOCK), :],
        )
        near_o[0, pl.ds(at, 2 * BLOCK), :] = found[:, :HALF]
        near_o[1, pl.ds(at, 2 * BLOCK), :] = found[:, HALF:]
        return 0

    lax.fori_loop(2, 3, near_pair, 0)

    remote(transfer_x.at[1 - side], transfer_x.at[1 - side], 0, 1, core).wait_recv()
    send_h1 = []
    for p in range(PIECES):
        for one in send_x[p]:
            one.wait_recv()
        c1 = dot_t(c0[piece(p), :], transfer[0, 0]) + dot_t(x_in[0, piece(p), :], transfer[0, 1])
        c1x = dot_t(x_in[1, piece(p), :], transfer_x[0]) + dot_t(x_in[2, piece(p), :], transfer_x[1])
        c2[piece(p), :] = (
            dot_t(c1.astype(BF16), transfer[1, 0]) + dot_t(c1x.astype(BF16), transfer[1, 1])
        ).astype(BF16)
        send_h1.append(remote(c2.at[piece(p)], h1_in.at[piece(p)], 7, p, h1))
        send_h1[p].start()

    lax.fori_loop(3, 6, near_pair, 0)

    @pl.when(n > 0)
    def _():
        halo_copy(1).wait_recv()

    @pl.when(n < 3)
    def _():
        halo_copy(0).wait_recv()

    lax.fori_loop(0, 1, near_pair, 0)

    send_h2 = []
    for p in range(PIECES):
        send_h1[p].wait_recv()
        c3[piece(p), :] = (
            dot_t(c2[piece(p), :], transfer[2, 0]) + dot_t(h1_in[piece(p), :], transfer[2, 1])
        ).astype(BF16)
        send_h2.append(remote(c3.at[piece(p)], h2_in.at[piece(p)], 8, p, h2))
        send_h2[p].start()

    lax.fori_loop(1, 2, near_pair, 0)
    lax.fori_loop(6, 8, near_pair, 0)
    loads[6].wait()

    def share(i, k, p, who):
        return remote(coarse.at[k, piece(p)], coarse.at[k, piece(p)], 9 + i, p, who)

    send_q = []
    for p in range(PIECES):
        send_h2[p].wait_recv()
        coarse[quarter, piece(p), :] = (
            dot_t(c3[piece(p), :], transfer[3, 0]) + dot_t(h2_in[piece(p), :], transfer[3, 1])
        ).astype(BF16)
        send_q += [share(i, quarter, p, who) for i, who in enumerate((zside, cross, core))]
        for one in send_q[-3:]:
            one.start()
    for p in range(PIECES):
        share(2, q1, p, core).wait_recv()

    held = coarse[pl.ds(2 * half, 2)].reshape(HALF, RANK)

    def far_rows(b, _):
        at = pl.ds(pl.multiple_of(b * OUT_ROWS, OUT_ROWS), OUT_ROWS)
        own_o[at, :] = (dot_t(out_basis[at, :], held) + near_o[half, at, :]).astype(BF16)
        return 0

    lax.fori_loop(0, ROWS // OUT_ROWS, far_rows, 0)

    send_tx.wait_send()
    pass_tx.wait_send()
    for one in (*send_c[0], *send_c[1], *send_x[0], *send_x[1], *send_h1, *send_h2, *send_q):
        one.wait_send()

    @pl.when(n < 3)
    def _():
        halo_copy(1).wait_send()

    @pl.when(n > 0)
    def _():
        halo_copy(0).wait_send()

    for p in range(PIECES):
        share(0, q2, p, zside).wait_recv()
        share(1, q3, p, cross).wait_recv()
    other_o[...] = coarse[pl.ds(2 - 2 * half, 2)].reshape(HALF, RANK)


def tree(order, cols, sources, basis, blocks, transfer, out_basis):
    quarter = (QUARTER, RANK)
    scratch = [
        VMEM((BLOCKS_DEV, BLOCK), I32),
        VMEM((NEAR, BLOCKS_DEV), I32),
        VMEM((ROWS, RHS), BF16),
        VMEM((ROWS, RANK), BF16),
        VMEM((BLOCKS_DEV, NEAR, BLOCK, BLOCK), BF16),
        VMEM((4, 2, RANK, RANK), BF16),
        VMEM((ROWS, RANK), BF16),
        VMEM((BLOCKS_DEV, BLOCK, BLOCK), I32),
        VMEM((16, 128), I32),
        SMEM((16, 128), I32),
        VMEM((ROWS, RANK), BF16),
        VMEM((ROWS + 2 * HALO, RHS), BF16),
        VMEM((2, *quarter), F32),
        VMEM((4, *quarter), BF16),
        VMEM((3, *quarter), BF16),
        VMEM(quarter, BF16),
        VMEM((3, *quarter), BF16),
        VMEM((2, RANK, RANK), BF16),
        VMEM(quarter, BF16),
        VMEM(quarter, BF16),
        VMEM(quarter, BF16),
        VMEM(quarter, BF16),
        VMEM((4, *quarter), BF16),
        DMA((7,)),
        DMA,
        DMA((12, PIECES)),
        DMA((12, PIECES)),
        DMA((2,)),
        DMA((2,)),
    ]
    return pl.pallas_call(
        tree_kernel,
        out_shape=(
            VMEM((HALF, RANK), BF16),
            VMEM((2, ROWS, HALF), F32),
            VMEM((ROWS, HALF), BF16),
        ),
        in_specs=[pl.BlockSpec(memory_space=pltpu.HBM)] * 7,
        out_specs=[pl.BlockSpec(memory_space=VMEM)] * 3,
        scratch_shapes=scratch,
        compiler_params=pltpu.CompilerParams(
            collective_id=0, has_side_effects=True, vmem_limit_bytes=44 << 20
        ),
        name="tree",
    )(order, cols, sources, basis, blocks, transfer, out_basis)


def far_kernel(basis, other, near, own, out_h, out, own_sem, store):
    count = ROWS // OUT_ROWS
    w, n = lax.axis_index("wide"), lax.axis_index("narrow")
    half = (flip(n, 2) * ((w // 8) % 2) + n * (1 - (w // 8) % 2)) // 2

    def columns(which):
        return pl.ds(pl.multiple_of(which * HALF, HALF), HALF)

    send_own = pltpu.make_async_copy(own, out_h.at[:, columns(half)], own_sem)
    send_own.start()
    stores = []
    for i in range(count):
        at = pl.ds(i * OUT_ROWS, OUT_ROWS)
        out[at, :] = (dot_t(basis[at, :], other[...]) + near[1 - half, at, :]).astype(BF16)
        stores.append(
            pltpu.make_async_copy(out.at[at], out_h.at[at, columns(1 - half)], store.at[i])
        )
        stores[-1].start()
    for one in stores:
        one.wait()
    send_own.wait()


def far(basis, other, near, own):
    return pl.pallas_call(
        far_kernel,
        out_shape=jax.ShapeDtypeStruct((ROWS, RHS), BF16),
        in_specs=[pl.BlockSpec(memory_space=VMEM)] * 4,
        out_specs=pl.BlockSpec(memory_space=pl.ANY),
        scratch_shapes=[VMEM((ROWS, HALF), BF16), DMA, DMA((ROWS // OUT_ROWS,))],
        compiler_params=pltpu.CompilerParams(vmem_limit_bytes=6 << 20),
        name="far",
    )(basis, other, near, own)


def on_device(sources, order, near_cols, near_blocks, in_basis, transfer, out_basis):
    given = (
        order.reshape(BLOCKS_DEV, BLOCK), near_cols.T, sources, in_basis, near_blocks, transfer[:, 0],
        out_basis,
    )
    other, near, own = tree(*(pltpu.with_memory_space_constraint(x, pltpu.HBM) for x in given))
    return far(out_basis, other, near, own)


def solution(mesh):
    return jax.shard_map(
        on_device,
        mesh=mesh,
        in_specs=(
            P(("wide", "narrow"), None),
            P(("wide", "narrow")),
            P(("wide", "narrow"), None),
            P(("wide", "narrow"), None, None, None),
            P(("wide", "narrow"), None),
            P(None, "wide", None, None, None),
            P(("wide", "narrow"), None),
        ),
        out_specs=P(("wide", "narrow"), None),
        check_vma=False,
    )
```

```python
import functools

import jax
import jax.numpy as jnp
from jax import lax
from jax.experimental import pallas as pl
from jax.experimental.pallas import tpu as pltpu
from jax.sharding import PartitionSpec as P

F32, BF16, I32 = jnp.float32, jnp.bfloat16, jnp.int32
MESH = pl.DeviceIdType.MESH
ROWS = 2048
RHS = 512
RANK = 256
BLOCK = 128
REACH = 4
NEAR = 8
BLOCKS_DEV = ROWS // BLOCK
OFFSETS = 2 * REACH + 1
CLUSTER_BLOCKS = 64
HALO = REACH * BLOCK
QUARTER = RHS // 4
HALF = RHS // 2
PIECES = 4
PIECE = QUARTER // PIECES
GATHER_ROWS = 512
OUT_ROWS = 512
LAST_ROWS = 256
SCATTER_ROWS = 1024
VMEM, SMEM, DMA = pltpu.VMEM, pltpu.SMEM, pltpu.SemaphoreType.DMA


def flip(index, bit):
    return index + bit - 2 * bit * ((index // bit) % 2)


def dot(a, b):
    return jnp.dot(a, b, preferred_element_type=F32)


def dot_t(a, b):
    return lax.dot_general(a, b, (((1,), (1,)), ((), ())), preferred_element_type=F32)


def level(own, partner, pair):
    return dot_t(
        jnp.concatenate([own, partner], axis=1), jnp.concatenate([pair[0], pair[1]], axis=1)
    ).astype(BF16)


def piece(p):
    return pl.ds(p * PIECE, PIECE)


def tree_kernel(
    order_h, cols_h, sources_h, basis_h, blocks_h, transfer_h, out_basis_h,
    other_o, near_o, own_o, out_basis,
    order, cols, sources, basis, blocks, transfer,
    order_col, table_v, table_s, moved, permuted, part, part_b, part_in,
    c0, x_in, transfer_x, c2, h1_in, c3, h2_in, coarse,
    load, table_sem, send, recv, halo_send, halo_recv,
):
    w, n = lax.axis_index("wide"), lax.axis_index("narrow")
    first_row = (w * 4 + n) * ROWS
    quarter = flip(n, 2) * ((w // 8) % 2) + n * (1 - (w // 8) % 2)
    core = (w, flip(n, 1))
    zside = (w, flip(n, 2))
    cross = (w, flip(flip(n, 1), 2))
    x1, x2, x3 = (flip(w, 1), n), (flip(w, 2), n), (flip(flip(w, 1), 2), n)
    h1, h2 = (flip(w, 4), n), (flip(w, 8), flip(n, 2))

    loads = [
        pltpu.make_async_copy(a, b, load.at[i])
        for i, (a, b) in enumerate(
            (
                (order_h, order),
                (basis_h, basis),
                (sources_h, sources),
                (transfer_h, transfer),
                (cols_h, cols),
                (blocks_h, blocks),
                (out_basis_h, out_basis),
            )
        )
    ]
    for one in loads[:2]:
        one.start()
    barrier = pltpu.get_barrier_semaphore()
    partners = (core, zside, cross, x1, x2, x3, h1, h2)
    for who in partners:
        pl.semaphore_signal(barrier, inc=1, device_id=who, device_id_type=MESH)

    def remote(src, dst, i, p, who):
        return pltpu.make_async_remote_copy(
            src_ref=src, dst_ref=dst, send_sem=send.at[i, p], recv_sem=recv.at[i, p],
            device_id=who, device_id_type=MESH,
        )

    loads[0].wait()
    loads[2].start()
    turned = order[...].T
    for k in range(BLOCKS_DEV):
        order_col[k] = jnp.broadcast_to(turned[:, k : k + 1], (BLOCK, BLOCK))
    loads[1].wait()
    for one in loads[3:]:
        one.start()

    def move(b, _):
        at = pl.multiple_of(b * SCATTER_ROWS, SCATTER_ROWS)
        ids = lax.broadcasted_iota(I32, (SCATTER_ROWS, BLOCK), 0) + (first_row + at)
        hot = jnp.concatenate(
            [jnp.where(ids == order[k : k + 1, :], 1.0, 0.0).astype(BF16) for k in range(BLOCKS_DEV)],
            axis=1,
        )
        moved[pl.ds(at, SCATTER_ROWS), :] = dot(hot, basis[...]).astype(BF16)
        return 0

    lax.fori_loop(0, ROWS // SCATTER_ROWS, move, 0)
    loads[3].wait()
    pl.semaphore_wait(barrier, len(partners))
    side = n % 2
    send_tx = remote(transfer.at[0, side], transfer_x.at[side], 0, 0, x2)
    send_tx.start()

    loads[2].wait()
    half = quarter // 2
    q1, q2 = flip(quarter, 1), flip(quarter, 2)
    q3 = flip(q1, 2)

    def half_term(which):
        columns = sources[:, pl.ds(pl.multiple_of(which * HALF, HALF), HALF)]
        return lax.dot_general(
            columns, moved[...], (((0,), (0,)), ((), ())), preferred_element_type=F32
        )

    pair = (2, QUARTER, RANK)
    part_b[pl.ds(2 - 2 * half, 2)] = half_term(1 - half).astype(BF16).reshape(pair)
    send_c = [
        [
            remote(part_b.at[k, piece(p)], part_in.at[i, piece(p)], 1 + i, p, who)
            for i, (k, who) in enumerate(((q2, zside), (q3, cross), (q1, core)))
        ]
        for p in range(PIECES)
    ]
    for p in range(PIECES):
        for one in send_c[p][:2]:
            one.start()
    term = half_term(half).reshape(pair)
    part[...] = term
    part_b[pl.ds(2 * half, 2)] = term.astype(BF16)
    for p in range(PIECES):
        send_c[p][2].start()

    def gather(b, _):
        lanes = lax.broadcasted_iota(I32, (BLOCK, BLOCK), 1) + first_row
        rows = []
        for k in range(GATHER_ROWS // BLOCK):
            ids = order_col[b * (GATHER_ROWS // BLOCK) + k]
            rows.append(
                jnp.concatenate(
                    [jnp.where(lanes + c * BLOCK == ids, 1.0, 0.0).astype(BF16) for c in range(BLOCKS_DEV)],
                    axis=1,
                )
            )
        hot = jnp.concatenate(rows, axis=0)
        at = pl.multiple_of(b * GATHER_ROWS + HALO, HALO)
        permuted[pl.ds(at, GATHER_ROWS), :] = dot(hot, sources[...]).astype(BF16)
        return 0

    first = 3 - 3 * (n // 2)
    gather(first, 0)

    def halo_copy(up):
        if up:
            src, dst, who = permuted.at[pl.ds(ROWS, HALO)], permuted.at[pl.ds(0, HALO)], (n + 1) % 4
        else:
            src, dst, who = permuted.at[pl.ds(HALO, HALO)], permuted.at[pl.ds(ROWS + HALO, HALO)], (n + 3) % 4
        return pltpu.make_async_remote_copy(
            src_ref=src, dst_ref=dst, send_sem=halo_send.at[up], recv_sem=halo_recv.at[up],
            device_id=(w, who), device_id_type=MESH,
        )

    @pl.when(n < 2)
    def _():
        halo_copy(1).start()

    @pl.when(n >= 2)
    def _():
        halo_copy(0).start()

    loads[4].wait()
    listed = cols[...]
    lane = lax.broadcasted_iota(I32, (NEAR, BLOCKS_DEV), 1)
    entry = lax.broadcasted_iota(I32, (NEAR, BLOCKS_DEV), 0)
    rank = jnp.zeros((NEAR, BLOCKS_DEV), I32)
    for e in range(NEAR - 1):
        same = jnp.where(listed == listed[e : e + 1, :], 1, 0)
        rank = rank + jnp.where(entry > e, same, 0)
    slot = listed - lane - (w * 4 + n) * BLOCKS_DEV + REACH
    slot = slot + jnp.where(listed == w * CLUSTER_BLOCKS, -rank, rank)
    for d in range(OFFSETS):
        table_v[d : d + 1, :BLOCKS_DEV] = jnp.sum(
            jnp.where(slot == d, entry + 1, 0), axis=0, keepdims=True
        )
    table_copy = pltpu.make_async_copy(table_v, table_s, table_sem)
    table_copy.start()

    send_x = []
    for p in range(PIECES):
        for one in send_c[p]:
            one.wait_recv()
        own = part[quarter % 2, piece(p), :]
        for i in range(3):
            own = own + part_in[i, piece(p), :].astype(F32)
        c0[piece(p), :] = own.astype(BF16)
        send_x.append(
            [
                remote(c0.at[piece(p)], x_in.at[i, piece(p)], 4 + i, p, who)
                for i, who in ((1, x2), (0, x1), (2, x3))
            ]
        )
        for one in send_x[p]:
            one.start()

    gather(3 - first, 0)

    @pl.when(n == 2)
    def _():
        halo_copy(1).start()

    @pl.when(n == 1)
    def _():
        halo_copy(0).start()

    @pl.when(n == 0)
    def _():
        for k in range(REACH):
            permuted[k * BLOCK : (k + 1) * BLOCK, :] = permuted[HALO : HALO + BLOCK, :]

    @pl.when(n == 3)
    def _():
        for k in range(REACH):
            at = ROWS + HALO + k * BLOCK
            permuted[at : at + BLOCK, :] = permuted[ROWS + HALO - BLOCK : ROWS + HALO, :]

    send_tx.wait_recv()
    pass_tx = remote(transfer_x.at[side], transfer_x.at[side], 0, 1, core)
    pass_tx.start()
    gather(1, 0)
    table_copy.wait()
    loads[5].wait()

    def near_pair(p, _):
        def row(r):
            found = []
            for d in range(OFFSETS):
                at = table_s[d, r]
                block = blocks[r, jnp.maximum(at - 1, 0)]
                found.append(jnp.where(at > 0, block, jnp.zeros_like(block)))
            return found

        none = jnp.zeros((BLOCK, BLOCK), BF16)
        upper = jnp.concatenate(row(2 * p) + [none], axis=1)
        lower = jnp.concatenate([none] + row(2 * p + 1), axis=1)
        at = pl.multiple_of(p * 2 * BLOCK, 2 * BLOCK)
        found = dot(
            jnp.concatenate([upper, lower], axis=0),
            permuted[pl.ds(at, (OFFSETS + 1) * BLOCK), :],
        )
        near_o[0, pl.ds(at, 2 * BLOCK), :] = found[:, :HALF]
        near_o[1, pl.ds(at, 2 * BLOCK), :] = found[:, HALF:]
        return 0

    remote(transfer_x.at[1 - side], transfer_x.at[1 - side], 0, 1, core).wait_recv()
    send_h1 = []
    for p in range(PIECES):
        for one in send_x[p]:
            one.wait_recv()
        c1 = level(c0[piece(p), :], x_in[0, piece(p), :], transfer[0])
        c1x = level(x_in[1, piece(p), :], x_in[2, piece(p), :], transfer_x[...])
        c2[piece(p), :] = level(c1, c1x, transfer[1])
        send_h1.append(remote(c2.at[piece(p)], h1_in.at[piece(p)], 7, p, h1))
        send_h1[p].start()

    gather(2, 0)
    lax.fori_loop(2, 5, near_pair, 0)

    send_h2 = []
    for p in range(PIECES):
        send_h1[p].wait_recv()
        c3[piece(p), :] = level(c2[piece(p), :], h1_in[piece(p), :], transfer[2])
        send_h2.append(remote(c3.at[piece(p)], h2_in.at[piece(p)], 8, p, h2))
        send_h2[p].start()

    lax.fori_loop(5, 6, near_pair, 0)

    @pl.when(n > 0)
    def _():
        halo_copy(1).wait_recv()

    @pl.when(n < 3)
    def _():
        halo_copy(0).wait_recv()

    lax.fori_loop(0, 2, near_pair, 0)
    lax.fori_loop(6, 8, near_pair, 0)
    loads[6].wait()

    def share(i, k, p, who):
        return remote(coarse.at[k, piece(p)], coarse.at[k, piece(p)], 9 + i, p, who)

    send_q = []
    for p in range(PIECES):
        send_h2[p].wait_recv()
        coarse[quarter, piece(p), :] = level(c3[piece(p), :], h2_in[piece(p), :], transfer[3])
        send_q += [share(i, quarter, p, who) for i, who in enumerate((zside, cross, core))]
        for one in send_q[-3:]:
            one.start()
    for p in range(PIECES):
        share(2, q1, p, core).wait_recv()

    held = coarse[pl.ds(2 * half, 2)].reshape(HALF, RANK)

    def far_rows(b, _):
        at = pl.ds(pl.multiple_of(b * OUT_ROWS, OUT_ROWS), OUT_ROWS)
        own_o[at, :] = (dot_t(out_basis[at, :], held) + near_o[half, at, :]).astype(BF16)
        return 0

    lax.fori_loop(0, ROWS // OUT_ROWS, far_rows, 0)

    send_tx.wait_send()
    pass_tx.wait_send()
    for one in (*sum(send_c, []), *sum(send_x, []), *send_h1, *send_h2, *send_q):
        one.wait_send()

    @pl.when(n < 3)
    def _():
        halo_copy(1).wait_send()

    @pl.when(n > 0)
    def _():
        halo_copy(0).wait_send()

    for p in range(PIECES):
        share(0, q2, p, zside).wait_recv()
        share(1, q3, p, cross).wait_recv()
    other_o[...] = coarse[pl.ds(2 - 2 * half, 2)].reshape(HALF, RANK)


def tree(order, cols, sources, basis, blocks, transfer, out_basis):
    quarter = (QUARTER, RANK)
    scratch = [
        VMEM((BLOCKS_DEV, BLOCK), I32),
        VMEM((NEAR, BLOCKS_DEV), I32),
        VMEM((ROWS, RHS), BF16),
        VMEM((ROWS, RANK), BF16),
        VMEM((BLOCKS_DEV, NEAR, BLOCK, BLOCK), BF16),
        VMEM((4, 2, RANK, RANK), BF16),
        VMEM((BLOCKS_DEV, BLOCK, BLOCK), I32),
        VMEM((16, 128), I32),
        SMEM((16, 128), I32),
        VMEM((ROWS, RANK), BF16),
        VMEM((ROWS + 2 * HALO, RHS), BF16),
        VMEM((2, *quarter), F32),
        VMEM((4, *quarter), BF16),
        VMEM((3, *quarter), BF16),
        VMEM(quarter, BF16),
        VMEM((3, *quarter), BF16),
        VMEM((2, RANK, RANK), BF16),
        VMEM(quarter, BF16),
        VMEM(quarter, BF16),
        VMEM(quarter, BF16),
        VMEM(quarter, BF16),
        VMEM((4, *quarter), BF16),
        DMA((7,)),
        DMA,
        DMA((12, PIECES)),
        DMA((12, PIECES)),
        DMA((2,)),
        DMA((2,)),
    ]
    return pl.pallas_call(
        tree_kernel,
        out_shape=(
            VMEM((HALF, RANK), BF16),
            VMEM((2, ROWS, HALF), F32),
            VMEM((ROWS, HALF), BF16),
            VMEM((ROWS, RANK), BF16),
        ),
        in_specs=[pl.BlockSpec(memory_space=pltpu.HBM)] * 7,
        out_specs=[pl.BlockSpec(memory_space=VMEM)] * 4,
        scratch_shapes=scratch,
        compiler_params=pltpu.CompilerParams(
            collective_id=0, has_side_effects=True, vmem_limit_bytes=44 << 20
        ),
        name="tree",
    )(order, cols, sources, basis, blocks, transfer, out_basis)


def far_kernel(basis, other, near, own, out_h, out, own_sem, store):
    count = ROWS // LAST_ROWS
    w, n = lax.axis_index("wide"), lax.axis_index("narrow")
    half = (flip(n, 2) * ((w // 8) % 2) + n * (1 - (w // 8) % 2)) // 2

    def columns(which):
        return pl.ds(pl.multiple_of(which * HALF, HALF), HALF)

    send_own = pltpu.make_async_copy(own, out_h.at[:, columns(half)], own_sem)
    send_own.start()
    stores = []
    for i in range(count):
        at = pl.ds(i * LAST_ROWS, LAST_ROWS)
        out[at, :] = (dot_t(basis[at, :], other[...]) + near[1 - half, at, :]).astype(BF16)
        stores.append(
            pltpu.make_async_copy(out.at[at], out_h.at[at, columns(1 - half)], store.at[i])
        )
        stores[-1].start()
    for one in stores:
        one.wait()
    send_own.wait()


def far(basis, other, near, own):
    return pl.pallas_call(
        far_kernel,
        out_shape=jax.ShapeDtypeStruct((ROWS, RHS), BF16),
        in_specs=[pl.BlockSpec(memory_space=VMEM)] * 4,
        out_specs=pl.BlockSpec(memory_space=pl.ANY),
        scratch_shapes=[VMEM((ROWS, HALF), BF16), DMA, DMA((ROWS // LAST_ROWS,))],
        compiler_params=pltpu.CompilerParams(vmem_limit_bytes=6 << 20),
        name="far",
    )(basis, other, near, own)


def on_device(sources, order, near_cols, near_blocks, in_basis, transfer, out_basis):
    given = (
        order.reshape(BLOCKS_DEV, BLOCK), near_cols.T, sources, in_basis, near_blocks, transfer[:, 0],
        out_basis,
    )
    other, near, own, basis = tree(*(pltpu.with_memory_space_constraint(x, pltpu.HBM) for x in given))
    return far(basis, other, near, own)


def solution(mesh):
    return jax.shard_map(
        on_device,
        mesh=mesh,
        in_specs=(
            P(("wide", "narrow"), None),
            P(("wide", "narrow")),
            P(("wide", "narrow"), None),
            P(("wide", "narrow"), None, None, None),
            P(("wide", "narrow"), None),
            P(None, "wide", None, None, None),
            P(("wide", "narrow"), None),
        ),
        out_specs=P(("wide", "narrow"), None),
        check_vma=False,
    )
```

```python
import functools

import jax
import jax.numpy as jnp
from jax import lax
from jax.experimental import pallas as pl
from jax.experimental.pallas import tpu as pltpu
from jax.sharding import PartitionSpec as P

F32, BF16, I32 = jnp.float32, jnp.bfloat16, jnp.int32
MESH = pl.DeviceIdType.MESH
ROWS = 2048
RHS = 512
RANK = 256
BLOCK = 128
REACH = 4
NEAR = 8
BLOCKS_DEV = ROWS // BLOCK
OFFSETS = 2 * REACH + 1
CLUSTER_BLOCKS = 64
HALO = REACH * BLOCK
QUARTER = RHS // 4
HALF = RHS // 2
PIECES = 4
PIECE = QUARTER // PIECES
OUT_ROWS = 512
LAST_ROWS = 256
SCATTER_ROWS = 1024
VMEM, SMEM, DMA = pltpu.VMEM, pltpu.SMEM, pltpu.SemaphoreType.DMA


def flip(index, bit):
    return index + bit - 2 * bit * ((index // bit) % 2)


def dot(a, b):
    return jnp.dot(a, b, preferred_element_type=F32)


def dot_t(a, b):
    return lax.dot_general(a, b, (((1,), (1,)), ((), ())), preferred_element_type=F32)


def level(own, partner, pair):
    return dot_t(
        jnp.concatenate([own, partner], axis=1), jnp.concatenate([pair[0], pair[1]], axis=1)
    ).astype(BF16)


def piece(p):
    return pl.ds(p * PIECE, PIECE)


def tree_kernel(
    order_h, cols_h, sources_h, basis_h, blocks_h, transfer_h, out_basis_h,
    other_o, near_o, own_o, out_basis,
    order, cols, sources, basis, blocks, transfer,
    order_col, table_v, table_s, moved, permuted, part, part_b, part_in,
    c0, x_in, transfer_x, c2, h1_in, c3, h2_in, coarse,
    load, table_sem, send, recv, halo_send, halo_recv,
):
    w, n = lax.axis_index("wide"), lax.axis_index("narrow")
    first_row = (w * 4 + n) * ROWS
    quarter = flip(n, 2) * ((w // 8) % 2) + n * (1 - (w // 8) % 2)
    core = (w, flip(n, 1))
    zside = (w, flip(n, 2))
    cross = (w, flip(flip(n, 1), 2))
    x1, x2, x3 = (flip(w, 1), n), (flip(w, 2), n), (flip(flip(w, 1), 2), n)
    h1, h2 = (flip(w, 4), n), (flip(w, 8), flip(n, 2))

    loads = [
        pltpu.make_async_copy(a, b, load.at[i])
        for i, (a, b) in enumerate(
            (
                (order_h, order),
                (basis_h, basis),
                (sources_h, sources),
                (transfer_h, transfer),
                (cols_h, cols),
                (blocks_h, blocks),
                (out_basis_h, out_basis),
            )
        )
    ]
    for one in loads[:2]:
        one.start()
    barrier = pltpu.get_barrier_semaphore()
    partners = (core, zside, cross, x1, x2, x3, h1, h2)
    for who in partners:
        pl.semaphore_signal(barrier, inc=1, device_id=who, device_id_type=MESH)

    def remote(src, dst, i, j, who):
        return pltpu.make_async_remote_copy(
            src_ref=src, dst_ref=dst, send_sem=send.at[i], recv_sem=recv.at[j],
            device_id=who, device_id_type=MESH,
        )

    loads[0].wait()
    loads[2].start()
    turned = order[...].T
    for k in range(BLOCKS_DEV):
        order_col[k] = jnp.broadcast_to(turned[:, k : k + 1], (BLOCK, BLOCK))
    loads[1].wait()
    for one in loads[3:]:
        one.start()

    def move(b, _):
        at = pl.multiple_of(b * SCATTER_ROWS, SCATTER_ROWS)
        ids = lax.broadcasted_iota(I32, (SCATTER_ROWS, BLOCK), 0) + (first_row + at)
        hot = jnp.concatenate(
            [jnp.where(ids == order[k : k + 1, :], 1.0, 0.0).astype(BF16) for k in range(BLOCKS_DEV)],
            axis=1,
        )
        moved[pl.ds(at, SCATTER_ROWS), :] = dot(hot, basis[...]).astype(BF16)
        return 0

    lax.fori_loop(0, ROWS // SCATTER_ROWS, move, 0)
    loads[3].wait()
    pl.semaphore_wait(barrier, len(partners))
    side = n % 2
    send_tx = remote(transfer.at[0, side], transfer_x.at[side], 0, 0, x2)
    send_tx.start()

    loads[2].wait()
    half = quarter // 2
    q1, q2 = flip(quarter, 1), flip(quarter, 2)
    q3 = flip(q1, 2)

    def half_term(which):
        columns = sources[:, pl.ds(pl.multiple_of(which * HALF, HALF), HALF)]
        return lax.dot_general(
            columns, moved[...], (((0,), (0,)), ((), ())), preferred_element_type=F32
        )

    pair = (2, QUARTER, RANK)
    part_b[pl.ds(2 - 2 * half, 2)] = half_term(1 - half).astype(BF16).reshape(pair)
    send_c = [
        [
            remote(part_b.at[k, piece(p)], part_in.at[i, piece(p)], 2, 4 + p, who)
            for i, (k, who) in enumerate(((q2, zside), (q3, cross), (q1, core)))
        ]
        for p in range(PIECES)
    ]
    for p in range(PIECES):
        for one in send_c[p][:2]:
            one.start()
    term = half_term(half).reshape(pair)
    part[...] = term
    part_b[pl.ds(2 * half, 2)] = term.astype(BF16)
    for p in range(PIECES):
        send_c[p][2].start()

    def gather(k0, count):
        lanes = lax.broadcasted_iota(I32, (BLOCK, BLOCK), 1) + first_row
        rows = []
        for k in range(count):
            ids = order_col[k0 + k]
            rows.append(
                jnp.concatenate(
                    [jnp.where(lanes + c * BLOCK == ids, 1.0, 0.0).astype(BF16) for c in range(BLOCKS_DEV)],
                    axis=1,
                )
            )
        hot = jnp.concatenate(rows, axis=0)
        at = pl.multiple_of(k0 * BLOCK + HALO, BLOCK)
        permuted[pl.ds(at, count * BLOCK), :] = dot(hot, sources[...]).astype(BF16)

    first = (BLOCKS_DEV - REACH) * (1 - n // 2)
    gather(first, REACH)

    def halo_copy(up):
        if up:
            src, dst, who = permuted.at[pl.ds(ROWS, HALO)], permuted.at[pl.ds(0, HALO)], (n + 1) % 4
        else:
            src, dst, who = permuted.at[pl.ds(HALO, HALO)], permuted.at[pl.ds(ROWS + HALO, HALO)], (n + 3) % 4
        return pltpu.make_async_remote_copy(
            src_ref=src, dst_ref=dst, send_sem=halo_send.at[up], recv_sem=halo_recv.at[up],
            device_id=(w, who), device_id_type=MESH,
        )

    @pl.when(n < 2)
    def _():
        halo_copy(1).start()

    @pl.when(n >= 2)
    def _():
        halo_copy(0).start()

    loads[4].wait()
    listed = cols[...]
    lane = lax.broadcasted_iota(I32, (NEAR, BLOCKS_DEV), 1)
    entry = lax.broadcasted_iota(I32, (NEAR, BLOCKS_DEV), 0)
    rank = jnp.zeros((NEAR, BLOCKS_DEV), I32)
    for e in range(NEAR - 1):
        same = jnp.where(listed == listed[e : e + 1, :], 1, 0)
        rank = rank + jnp.where(entry > e, same, 0)
    slot = listed - lane - (w * 4 + n) * BLOCKS_DEV + REACH
    slot = slot + jnp.where(listed == w * CLUSTER_BLOCKS, -rank, rank)
    for d in range(OFFSETS):
        table_v[d : d + 1, :BLOCKS_DEV] = jnp.sum(
            jnp.where(slot == d, entry + 1, 0), axis=0, keepdims=True
        )
    table_copy = pltpu.make_async_copy(table_v, table_s, table_sem)
    table_copy.start()

    gather(BLOCKS_DEV - REACH - first, REACH)

    @pl.when(n == 2)
    def _():
        halo_copy(1).start()

    @pl.when(n == 1)
    def _():
        halo_copy(0).start()

    send_x = []
    for p in range(PIECES):
        remote(part_in.at[:, piece(p)], part_in.at[:, piece(p)], 2, 4 + p, core).wait_recv()
        own = part[quarter % 2, piece(p), :]
        for i in range(3):
            own = own + part_in[i, piece(p), :].astype(F32)
        c0[piece(p), :] = own.astype(BF16)
        send_x.append(
            [
                remote(c0.at[piece(p)], x_in.at[i, piece(p)], 3, 4 + PIECES + p, who)
                for i, who in ((1, x2), (0, x1), (2, x3))
            ]
        )
        for one in send_x[p]:
            one.start()
        if p < PIECES - 1:
            gather(REACH + p, 1)

    @pl.when(n == 0)
    def _():
        for k in range(REACH):
            permuted[k * BLOCK : (k + 1) * BLOCK, :] = permuted[HALO : HALO + BLOCK, :]

    @pl.when(n == 3)
    def _():
        for k in range(REACH):
            at = ROWS + HALO + k * BLOCK
            permuted[at : at + BLOCK, :] = permuted[ROWS + HALO - BLOCK : ROWS + HALO, :]

    send_tx.wait_recv()
    pass_tx = remote(transfer_x.at[side], transfer_x.at[side], 1, 1, core)
    pass_tx.start()
    gather(2 * REACH - 1, 1)
    gather(2 * REACH, REACH)
    table_copy.wait()
    loads[5].wait()

    def near_pair(p, _):
        def row(r):
            found = []
            for d in range(OFFSETS):
                at = table_s[d, r]
                block = blocks[r, jnp.maximum(at - 1, 0)]
                found.append(jnp.where(at > 0, block, jnp.zeros_like(block)))
            return found

        none = jnp.zeros((BLOCK, BLOCK), BF16)
        upper = jnp.concatenate(row(2 * p) + [none], axis=1)
        lower = jnp.concatenate([none] + row(2 * p + 1), axis=1)
        at = pl.multiple_of(p * 2 * BLOCK, 2 * BLOCK)
        found = dot(
            jnp.concatenate([upper, lower], axis=0),
            permuted[pl.ds(at, (OFFSETS + 1) * BLOCK), :],
        )
        near_o[0, pl.ds(at, 2 * BLOCK), :] = found[:, :HALF]
        near_o[1, pl.ds(at, 2 * BLOCK), :] = found[:, HALF:]
        return 0

    remote(transfer_x.at[1 - side], transfer_x.at[1 - side], 1, 1, core).wait_recv()
    send_h1 = []
    for p in range(PIECES):
        remote(x_in.at[:, piece(p)], x_in.at[:, piece(p)], 3, 4 + PIECES + p, x1).wait_recv()
        c1 = level(c0[piece(p), :], x_in[0, piece(p), :], transfer[0])
        c1x = level(x_in[1, piece(p), :], x_in[2, piece(p), :], transfer_x[...])
        c2[piece(p), :] = level(c1, c1x, transfer[1])
        send_h1.append(remote(c2.at[piece(p)], h1_in.at[piece(p)], 4, 4 + 2 * PIECES + p, h1))
        send_h1[p].start()

    lax.fori_loop(2, 5, near_pair, 0)

    send_h2 = []
    for p in range(PIECES):
        send_h1[p].wait_recv()
        c3[piece(p), :] = level(c2[piece(p), :], h1_in[piece(p), :], transfer[2])
        send_h2.append(remote(c3.at[piece(p)], h2_in.at[piece(p)], 5, 4 + 3 * PIECES + p, h2))
        send_h2[p].start()

    lax.fori_loop(5, 6, near_pair, 0)

    @pl.when(n > 0)
    def _():
        halo_copy(1).wait_recv()

    @pl.when(n < 3)
    def _():
        halo_copy(0).wait_recv()

    lax.fori_loop(0, 2, near_pair, 0)
    lax.fori_loop(6, 8, near_pair, 0)
    loads[6].wait()

    def share(i, k, p, who):
        return remote(coarse.at[k, piece(p)], coarse.at[k, piece(p)], 6, 2 + i // 2, who)

    send_q = []
    for p in range(PIECES):
        send_h2[p].wait_recv()
        coarse[quarter, piece(p), :] = level(c3[piece(p), :], h2_in[piece(p), :], transfer[3])
        send_q += [share(i, quarter, p, who) for i, who in enumerate((zside, cross, core))]
        for one in send_q[-3:]:
            one.start()
    remote(coarse.at[q1], coarse.at[q1], 6, 3, core).wait_recv()

    held = coarse[pl.ds(2 * half, 2)].reshape(HALF, RANK)

    def far_rows(b, _):
        at = pl.ds(pl.multiple_of(b * OUT_ROWS, OUT_ROWS), OUT_ROWS)
        own_o[at, :] = (dot_t(out_basis[at, :], held) + near_o[half, at, :]).astype(BF16)
        return 0

    lax.fori_loop(0, ROWS // OUT_ROWS, far_rows, 0)

    send_tx.wait_send()
    pass_tx.wait_send()
    remote(part_in, part_in, 2, 4, core).wait_send()
    remote(x_in, x_in, 3, 4, x1).wait_send()
    remote(c2, h1_in, 4, 4, h1).wait_send()
    remote(c3, h2_in, 5, 4, h2).wait_send()
    remote(part_in, part_in, 6, 4, core).wait_send()

    @pl.when(n < 3)
    def _():
        halo_copy(1).wait_send()

    @pl.when(n > 0)
    def _():
        halo_copy(0).wait_send()

    far_half = coarse.at[pl.ds(2 - 2 * half, 2)]
    remote(far_half, far_half, 6, 2, zside).wait_recv()
    other_o[...] = coarse[pl.ds(2 - 2 * half, 2)].reshape(HALF, RANK)


def tree(order, cols, sources, basis, blocks, transfer, out_basis):
    quarter = (QUARTER, RANK)
    scratch = [
        VMEM((BLOCKS_DEV, BLOCK), I32),
        VMEM((NEAR, BLOCKS_DEV), I32),
        VMEM((ROWS, RHS), BF16),
        VMEM((ROWS, RANK), BF16),
        VMEM((BLOCKS_DEV, NEAR, BLOCK, BLOCK), BF16),
        VMEM((4, 2, RANK, RANK), BF16),
        VMEM((BLOCKS_DEV, BLOCK, BLOCK), I32),
        VMEM((16, 128), I32),
        SMEM((16, 128), I32),
        VMEM((ROWS, RANK), BF16),
        VMEM((ROWS + 2 * HALO, RHS), BF16),
        VMEM((2, *quarter), F32),
        VMEM((4, *quarter), BF16),
        VMEM((3, *quarter), BF16),
        VMEM(quarter, BF16),
        VMEM((3, *quarter), BF16),
        VMEM((2, RANK, RANK), BF16),
        VMEM(quarter, BF16),
        VMEM(quarter, BF16),
        VMEM(quarter, BF16),
        VMEM(quarter, BF16),
        VMEM((4, *quarter), BF16),
        DMA((7,)),
        DMA,
        DMA((7,)),
        DMA((4 + 4 * PIECES,)),
        DMA((2,)),
        DMA((2,)),
    ]
    return pl.pallas_call(
        tree_kernel,
        out_shape=(
            VMEM((HALF, RANK), BF16),
            VMEM((2, ROWS, HALF), F32),
            VMEM((ROWS, HALF), BF16),
            VMEM((ROWS, RANK), BF16),
        ),
        in_specs=[pl.BlockSpec(memory_space=pltpu.HBM)] * 7,
        out_specs=[pl.BlockSpec(memory_space=VMEM)] * 4,
        scratch_shapes=scratch,
        compiler_params=pltpu.CompilerParams(
            collective_id=0, has_side_effects=True, vmem_limit_bytes=44 << 20
        ),
        name="tree",
    )(order, cols, sources, basis, blocks, transfer, out_basis)


def far_kernel(basis, other, near, own, out_h, out, own_sem, store):
    count = ROWS // LAST_ROWS
    w, n = lax.axis_index("wide"), lax.axis_index("narrow")
    half = (flip(n, 2) * ((w // 8) % 2) + n * (1 - (w // 8) % 2)) // 2

    def columns(which):
        return pl.ds(pl.multiple_of(which * HALF, HALF), HALF)

    send_own = pltpu.make_async_copy(own, out_h.at[:, columns(half)], own_sem)
    send_own.start()
    stores = []
    for i in range(count):
        at = pl.ds(i * LAST_ROWS, LAST_ROWS)
        out[at, :] = (dot_t(basis[at, :], other[...]) + near[1 - half, at, :]).astype(BF16)
        stores.append(
            pltpu.make_async_copy(out.at[at], out_h.at[at, columns(1 - half)], store.at[i])
        )
        stores[-1].start()
    for one in stores:
        one.wait()
    send_own.wait()


def far(basis, other, near, own):
    return pl.pallas_call(
        far_kernel,
        out_shape=jax.ShapeDtypeStruct((ROWS, RHS), BF16),
        in_specs=[pl.BlockSpec(memory_space=VMEM)] * 4,
        out_specs=pl.BlockSpec(memory_space=pl.ANY),
        scratch_shapes=[VMEM((ROWS, HALF), BF16), DMA, DMA((ROWS // LAST_ROWS,))],
        compiler_params=pltpu.CompilerParams(vmem_limit_bytes=6 << 20),
        name="far",
    )(basis, other, near, own)


def on_device(sources, order, near_cols, near_blocks, in_basis, transfer, out_basis):
    given = (
        order.reshape(BLOCKS_DEV, BLOCK), near_cols.T, sources, in_basis, near_blocks, transfer[:, 0],
        out_basis,
    )
    other, near, own, basis = tree(*(pltpu.with_memory_space_constraint(x, pltpu.HBM) for x in given))
    return far(basis, other, near, own)


def solution(mesh):
    return jax.shard_map(
        on_device,
        mesh=mesh,
        in_specs=(
            P(("wide", "narrow"), None),
            P(("wide", "narrow")),
            P(("wide", "narrow"), None),
            P(("wide", "narrow"), None, None, None),
            P(("wide", "narrow"), None),
            P(None, "wide", None, None, None),
            P(("wide", "narrow"), None),
        ),
        out_specs=P(("wide", "narrow"), None),
        check_vma=False,
    )
```

```python
import functools

import jax
import jax.numpy as jnp
from jax import lax
from jax.experimental import pallas as pl
from jax.experimental.pallas import tpu as pltpu
from jax.sharding import PartitionSpec as P

F32, BF16, I32 = jnp.float32, jnp.bfloat16, jnp.int32
MESH = pl.DeviceIdType.MESH
ROWS = 2048
RHS = 512
RANK = 256
BLOCK = 128
REACH = 4
NEAR = 8
BLOCKS_DEV = ROWS // BLOCK
OFFSETS = 2 * REACH + 1
CLUSTER_BLOCKS = 64
HALO = REACH * BLOCK
QUARTER = RHS // 4
HALF = RHS // 2
PIECES = 4
PIECE = QUARTER // PIECES
OUT_ROWS = 512
LAST_ROWS = 256
SCATTER_ROWS = 1024
VMEM, SMEM, DMA = pltpu.VMEM, pltpu.SMEM, pltpu.SemaphoreType.DMA


def flip(index, bit):
    return index + bit - 2 * bit * ((index // bit) % 2)


def dot(a, b):
    return jnp.dot(a, b, preferred_element_type=F32)


def dot_t(a, b):
    return lax.dot_general(a, b, (((1,), (1,)), ((), ())), preferred_element_type=F32)


def level(own, partner, pair):
    return dot_t(
        jnp.concatenate([own, partner], axis=1), jnp.concatenate([pair[0], pair[1]], axis=1)
    ).astype(BF16)


def piece(p):
    return pl.ds(p * PIECE, PIECE)


def tree_kernel(
    order_h, cols_h, sources_h, basis_h, blocks_h, transfer_h, out_basis_h,
    other_o, near_o, own_o, out_basis,
    order, cols, sources, basis, blocks, transfer,
    order_col, table_v, table_s, moved, permuted, part, part_b, part_in,
    c0, x_in, transfer_x, c2, h1_in, c3, h2_in, coarse,
    load, table_sem, send, recv, halo_send, halo_recv,
):
    w, n = lax.axis_index("wide"), lax.axis_index("narrow")
    first_row = (w * 4 + n) * ROWS
    quarter = flip(n, 2) * ((w // 8) % 2) + n * (1 - (w // 8) % 2)
    core = (w, flip(n, 1))
    zside = (w, flip(n, 2))
    cross = (w, flip(flip(n, 1), 2))
    x1, x2, x3 = (flip(w, 1), n), (flip(w, 2), n), (flip(flip(w, 1), 2), n)
    h1, h2 = (flip(w, 4), n), (flip(w, 8), flip(n, 2))

    loads = [
        pltpu.make_async_copy(a, b, load.at[i])
        for i, (a, b) in enumerate(
            (
                (order_h, order),
                (basis_h, basis),
                (sources_h, sources),
                (transfer_h, transfer),
                (cols_h, cols),
                (blocks_h, blocks),
                (out_basis_h, out_basis),
            )
        )
    ]
    for one in loads[:2]:
        one.start()
    barrier = pltpu.get_barrier_semaphore()
    partners = (core, zside, cross, x1, x2, x3, h1, h2)
    for who in partners:
        pl.semaphore_signal(barrier, inc=1, device_id=who, device_id_type=MESH)

    def remote(src, dst, i, j, who):
        return pltpu.make_async_remote_copy(
            src_ref=src, dst_ref=dst, send_sem=send.at[i], recv_sem=recv.at[j],
            device_id=who, device_id_type=MESH,
        )

    loads[0].wait()
    loads[2].start()
    turned = order[...].T
    for k in range(BLOCKS_DEV):
        order_col[k] = jnp.broadcast_to(turned[:, k : k + 1], (BLOCK, BLOCK))
    loads[1].wait()
    for one in loads[3:]:
        one.start()

    def move(b, _):
        at = pl.multiple_of(b * SCATTER_ROWS, SCATTER_ROWS)
        ids = lax.broadcasted_iota(I32, (SCATTER_ROWS, BLOCK), 0) + (first_row + at)
        hot = jnp.concatenate(
            [jnp.where(ids == order[k : k + 1, :], 1.0, 0.0).astype(BF16) for k in range(BLOCKS_DEV)],
            axis=1,
        )
        moved[pl.ds(at, SCATTER_ROWS), :] = dot(hot, basis[...]).astype(BF16)
        return 0

    lax.fori_loop(0, ROWS // SCATTER_ROWS, move, 0)
    loads[3].wait()
    pl.semaphore_wait(barrier, len(partners))
    side = n % 2
    send_tx = remote(transfer.at[0, side], transfer_x.at[side], 0, 0, x2)
    send_tx.start()

    loads[2].wait()
    half = quarter // 2
    q1, q2 = flip(quarter, 1), flip(quarter, 2)
    q3 = flip(q1, 2)

    def half_term(which):
        columns = sources[:, pl.ds(pl.multiple_of(which * HALF, HALF), HALF)]
        return lax.dot_general(
            columns, moved[...], (((0,), (0,)), ((), ())), preferred_element_type=F32
        )

    pair = (2, QUARTER, RANK)
    part_b[pl.ds(2 - 2 * half, 2)] = half_term(1 - half).astype(BF16).reshape(pair)
    send_c = [
        [
            remote(part_b.at[k, piece(p)], part_in.at[i, piece(p)], 2, 4 + p, who)
            for i, (k, who) in enumerate(((q2, zside), (q3, cross), (q1, core)))
        ]
        for p in range(PIECES)
    ]
    for p in range(PIECES):
        for one in send_c[p][:2]:
            one.start()
    term = half_term(half).reshape(pair)
    part[...] = term
    part_b[pl.ds(2 * half, 2)] = term.astype(BF16)
    for p in range(PIECES):
        send_c[p][2].start()

    def gather(k0, count):
        lanes = lax.broadcasted_iota(I32, (BLOCK, BLOCK), 1) + first_row
        rows = []
        for k in range(count):
            ids = order_col[k0 + k]
            rows.append(
                jnp.concatenate(
                    [jnp.where(lanes + c * BLOCK == ids, 1.0, 0.0).astype(BF16) for c in range(BLOCKS_DEV)],
                    axis=1,
                )
            )
        hot = jnp.concatenate(rows, axis=0)
        at = pl.multiple_of(k0 * BLOCK + HALO, BLOCK)
        permuted[pl.ds(at, count * BLOCK), :] = dot(hot, sources[...]).astype(BF16)

    first = (BLOCKS_DEV - REACH) * (1 - n // 2)
    gather(first, REACH)

    def halo_copy(up):
        if up:
            src, dst, who = permuted.at[pl.ds(ROWS, HALO)], permuted.at[pl.ds(0, HALO)], (n + 1) % 4
        else:
            src, dst, who = permuted.at[pl.ds(HALO, HALO)], permuted.at[pl.ds(ROWS + HALO, HALO)], (n + 3) % 4
        return pltpu.make_async_remote_copy(
            src_ref=src, dst_ref=dst, send_sem=halo_send.at[up], recv_sem=halo_recv.at[up],
            device_id=(w, who), device_id_type=MESH,
        )

    @pl.when(n < 2)
    def _():
        halo_copy(1).start()

    @pl.when(n >= 2)
    def _():
        halo_copy(0).start()

    loads[4].wait()
    listed = cols[...]
    lane = lax.broadcasted_iota(I32, (NEAR, BLOCKS_DEV), 1)
    entry = lax.broadcasted_iota(I32, (NEAR, BLOCKS_DEV), 0)
    rank = jnp.zeros((NEAR, BLOCKS_DEV), I32)
    for e in range(NEAR - 1):
        same = jnp.where(listed == listed[e : e + 1, :], 1, 0)
        rank = rank + jnp.where(entry > e, same, 0)
    slot = listed - lane - (w * 4 + n) * BLOCKS_DEV + REACH
    slot = slot + jnp.where(listed == w * CLUSTER_BLOCKS, -rank, rank)
    for d in range(OFFSETS):
        table_v[d : d + 1, :BLOCKS_DEV] = jnp.sum(
            jnp.where(slot == d, entry + 1, 0), axis=0, keepdims=True
        )
    table_copy = pltpu.make_async_copy(table_v, table_s, table_sem)
    table_copy.start()

    gather(BLOCKS_DEV - REACH - first, REACH)

    @pl.when(n == 2)
    def _():
        halo_copy(1).start()

    @pl.when(n == 1)
    def _():
        halo_copy(0).start()

    send_x = []
    for p in range(PIECES):
        remote(part_in.at[:, piece(p)], part_in.at[:, piece(p)], 2, 4 + p, core).wait_recv()
        own = part[quarter % 2, piece(p), :]
        for i in range(3):
            own = own + part_in[i, piece(p), :].astype(F32)
        c0[piece(p), :] = own.astype(BF16)
        send_x.append(
            [
                remote(c0.at[piece(p)], x_in.at[i, piece(p)], 3, 4 + PIECES + p, who)
                for i, who in ((1, x2), (0, x1), (2, x3))
            ]
        )
        for one in send_x[p]:
            one.start()
        if p < PIECES - 1:
            gather(REACH + p, 1)

    @pl.when(n == 0)
    def _():
        for k in range(REACH):
            permuted[k * BLOCK : (k + 1) * BLOCK, :] = permuted[HALO : HALO + BLOCK, :]

    @pl.when(n == 3)
    def _():
        for k in range(REACH):
            at = ROWS + HALO + k * BLOCK
            permuted[at : at + BLOCK, :] = permuted[ROWS + HALO - BLOCK : ROWS + HALO, :]

    send_tx.wait_recv()
    pass_tx = remote(transfer_x.at[side], transfer_x.at[side], 1, 1, core)
    pass_tx.start()
    gather(2 * REACH - 1, 1)
    gather(2 * REACH, REACH)
    table_copy.wait()
    loads[5].wait()

    def near_pair(p, _):
        def row(r):
            found = []
            for d in range(OFFSETS):
                at = table_s[d, r]
                block = blocks[r, jnp.maximum(at - 1, 0)]
                found.append(jnp.where(at > 0, block, jnp.zeros_like(block)))
            return found

        none = jnp.zeros((BLOCK, BLOCK), BF16)
        upper = jnp.concatenate(row(2 * p) + [none], axis=1)
        lower = jnp.concatenate([none] + row(2 * p + 1), axis=1)
        at = pl.multiple_of(p * 2 * BLOCK, 2 * BLOCK)
        found = dot(
            jnp.concatenate([upper, lower], axis=0),
            permuted[pl.ds(at, (OFFSETS + 1) * BLOCK), :],
        )
        near_o[0, pl.ds(at, 2 * BLOCK), :] = found[:, :HALF]
        near_o[1, pl.ds(at, 2 * BLOCK), :] = found[:, HALF:]
        return 0

    remote(transfer_x.at[1 - side], transfer_x.at[1 - side], 1, 1, core).wait_recv()
    send_h1 = []
    for p in range(PIECES):
        remote(x_in.at[:, piece(p)], x_in.at[:, piece(p)], 3, 4 + PIECES + p, x1).wait_recv()
        c1 = level(c0[piece(p), :], x_in[0, piece(p), :], transfer[0])
        c1x = level(x_in[1, piece(p), :], x_in[2, piece(p), :], transfer_x[...])
        c2[piece(p), :] = level(c1, c1x, transfer[1])
        send_h1.append(remote(c2.at[piece(p)], h1_in.at[piece(p)], 4, 4 + 2 * PIECES + p, h1))
        send_h1[p].start()

    lax.fori_loop(2, 4, near_pair, 0)

    send_h2 = []
    for p in range(PIECES):
        send_h1[p].wait_recv()
        c3[piece(p), :] = level(c2[piece(p), :], h1_in[piece(p), :], transfer[2])
        send_h2.append(remote(c3.at[piece(p)], h2_in.at[piece(p)], 5, 4 + 3 * PIECES + p, h2))
        send_h2[p].start()

    lax.fori_loop(4, 6, near_pair, 0)

    @pl.when(n > 0)
    def _():
        halo_copy(1).wait_recv()

    @pl.when(n < 3)
    def _():
        halo_copy(0).wait_recv()

    lax.fori_loop(0, 2, near_pair, 0)
    lax.fori_loop(6, 8, near_pair, 0)
    loads[6].wait()

    def share(i, k, p, who):
        return remote(coarse.at[k, piece(p)], coarse.at[k, piece(p)], 6, 2 + i // 2, who)

    send_q = []
    for p in range(PIECES):
        send_h2[p].wait_recv()
        coarse[quarter, piece(p), :] = level(c3[piece(p), :], h2_in[piece(p), :], transfer[3])
        send_q += [share(i, quarter, p, who) for i, who in enumerate((zside, cross, core))]
        for one in send_q[-3:]:
            one.start()
    remote(coarse.at[q1], coarse.at[q1], 6, 3, core).wait_recv()

    held = coarse[pl.ds(2 * half, 2)].reshape(HALF, RANK)

    def far_rows(b, _):
        at = pl.ds(pl.multiple_of(b * OUT_ROWS, OUT_ROWS), OUT_ROWS)
        own_o[at, :] = (dot_t(out_basis[at, :], held) + near_o[half, at, :]).astype(BF16)
        return 0

    lax.fori_loop(0, ROWS // OUT_ROWS, far_rows, 0)

    send_tx.wait_send()
    pass_tx.wait_send()
    remote(part_in, part_in, 2, 4, core).wait_send()
    remote(x_in, x_in, 3, 4, x1).wait_send()
    remote(c2, h1_in, 4, 4, h1).wait_send()
    remote(c3, h2_in, 5, 4, h2).wait_send()
    remote(part_in, part_in, 6, 4, core).wait_send()

    @pl.when(n < 3)
    def _():
        halo_copy(1).wait_send()

    @pl.when(n > 0)
    def _():
        halo_copy(0).wait_send()

    far_half = coarse.at[pl.ds(2 - 2 * half, 2)]
    remote(far_half, far_half, 6, 2, zside).wait_recv()
    other_o[...] = coarse[pl.ds(2 - 2 * half, 2)].reshape(HALF, RANK)


def tree(order, cols, sources, basis, blocks, transfer, out_basis):
    quarter = (QUARTER, RANK)
    scratch = [
        VMEM((BLOCKS_DEV, BLOCK), I32),
        VMEM((NEAR, BLOCKS_DEV), I32),
        VMEM((ROWS, RHS), BF16),
        VMEM((ROWS, RANK), BF16),
        VMEM((BLOCKS_DEV, NEAR, BLOCK, BLOCK), BF16),
        VMEM((4, 2, RANK, RANK), BF16),
        VMEM((BLOCKS_DEV, BLOCK, BLOCK), I32),
        VMEM((16, 128), I32),
        SMEM((16, 128), I32),
        VMEM((ROWS, RANK), BF16),
        VMEM((ROWS + 2 * HALO, RHS), BF16),
        VMEM((2, *quarter), F32),
        VMEM((4, *quarter), BF16),
        VMEM((3, *quarter), BF16),
        VMEM(quarter, BF16),
        VMEM((3, *quarter), BF16),
        VMEM((2, RANK, RANK), BF16),
        VMEM(quarter, BF16),
        VMEM(quarter, BF16),
        VMEM(quarter, BF16),
        VMEM(quarter, BF16),
        VMEM((4, *quarter), BF16),
        DMA((7,)),
        DMA,
        DMA((7,)),
        DMA((4 + 4 * PIECES,)),
        DMA((2,)),
        DMA((2,)),
    ]
    return pl.pallas_call(
        tree_kernel,
        out_shape=(
            VMEM((HALF, RANK), BF16),
            VMEM((2, ROWS, HALF), F32),
            VMEM((ROWS, HALF), BF16),
            VMEM((ROWS, RANK), BF16),
        ),
        in_specs=[pl.BlockSpec(memory_space=pltpu.HBM)] * 7,
        out_specs=[pl.BlockSpec(memory_space=VMEM)] * 4,
        scratch_shapes=scratch,
        compiler_params=pltpu.CompilerParams(
            collective_id=0, has_side_effects=True, vmem_limit_bytes=44 << 20
        ),
        name="tree",
    )(order, cols, sources, basis, blocks, transfer, out_basis)


def far_kernel(basis, other, near, own, out_h, out, own_sem, store):
    count = ROWS // LAST_ROWS
    w, n = lax.axis_index("wide"), lax.axis_index("narrow")
    half = (flip(n, 2) * ((w // 8) % 2) + n * (1 - (w // 8) % 2)) // 2

    def columns(which):
        return pl.ds(pl.multiple_of(which * HALF, HALF), HALF)

    send_own = pltpu.make_async_copy(own, out_h.at[:, columns(half)], own_sem)
    send_own.start()
    stores = []
    for i in range(count):
        at = pl.ds(i * LAST_ROWS, LAST_ROWS)
        out[at, :] = (dot_t(basis[at, :], other[...]) + near[1 - half, at, :]).astype(BF16)
        stores.append(
            pltpu.make_async_copy(out.at[at], out_h.at[at, columns(1 - half)], store.at[i])
        )
        stores[-1].start()
    for one in stores:
        one.wait()
    send_own.wait()


def far(basis, other, near, own):
    return pl.pallas_call(
        far_kernel,
        out_shape=jax.ShapeDtypeStruct((ROWS, RHS), BF16),
        in_specs=[pl.BlockSpec(memory_space=VMEM)] * 4,
        out_specs=pl.BlockSpec(memory_space=pl.ANY),
        scratch_shapes=[VMEM((ROWS, HALF), BF16), DMA, DMA((ROWS // LAST_ROWS,))],
        compiler_params=pltpu.CompilerParams(vmem_limit_bytes=6 << 20),
        name="far",
    )(basis, other, near, own)


def on_device(sources, order, near_cols, near_blocks, in_basis, transfer, out_basis):
    given = (
        order.reshape(BLOCKS_DEV, BLOCK), near_cols.T, sources, in_basis, near_blocks, transfer[:, 0],
        out_basis,
    )
    other, near, own, basis = tree(*(pltpu.with_memory_space_constraint(x, pltpu.HBM) for x in given))
    return far(basis, other, near, own)


def solution(mesh):
    return jax.shard_map(
        on_device,
        mesh=mesh,
        in_specs=(
            P(("wide", "narrow"), None),
            P(("wide", "narrow")),
            P(("wide", "narrow"), None),
            P(("wide", "narrow"), None, None, None),
            P(("wide", "narrow"), None),
            P(None, "wide", None, None, None),
            P(("wide", "narrow"), None),
        ),
        out_specs=P(("wide", "narrow"), None),
        check_vma=False,
    )
```

```python
import functools

import jax
import jax.numpy as jnp
from jax import lax
from jax.experimental import pallas as pl
from jax.experimental.pallas import tpu as pltpu
from jax.sharding import PartitionSpec as P

F32, BF16, I32 = jnp.float32, jnp.bfloat16, jnp.int32
MESH = pl.DeviceIdType.MESH
ROWS = 2048
RHS = 512
RANK = 256
BLOCK = 128
REACH = 4
NEAR = 8
BLOCKS_DEV = ROWS // BLOCK
OFFSETS = 2 * REACH + 1
CLUSTER_BLOCKS = 64
HALO = REACH * BLOCK
QUARTER = RHS // 4
HALF = RHS // 2
PIECES = 4
PIECE = QUARTER // PIECES
OUT_ROWS = 512
LAST_ROWS = 256
SCATTER_ROWS = 1024
VMEM, SMEM, DMA = pltpu.VMEM, pltpu.SMEM, pltpu.SemaphoreType.DMA


def flip(index, bit):
    return index + bit - 2 * bit * ((index // bit) % 2)


def dot(a, b):
    return jnp.dot(a, b, preferred_element_type=F32)


def dot_t(a, b):
    return lax.dot_general(a, b, (((1,), (1,)), ((), ())), preferred_element_type=F32)


def level(own, partner, pair):
    return dot_t(
        jnp.concatenate([own, partner], axis=1), jnp.concatenate([pair[0], pair[1]], axis=1)
    ).astype(BF16)


def piece(p):
    return pl.ds(p * PIECE, PIECE)


def tree_kernel(
    order_h, cols_h, sources_h, basis_h, blocks_h, transfer_h, out_basis_h,
    other_o, near_o, own_o, out_basis,
    order, cols, sources, basis, blocks, transfer,
    order_col, table_v, table_s, moved, permuted, part, part_b, part_in,
    c0, x_in, transfer_x, c2, h1_in, c3, h2_in, coarse,
    load, table_sem, send, recv, halo_send, halo_recv,
):
    w, n = lax.axis_index("wide"), lax.axis_index("narrow")
    first_row = (w * 4 + n) * ROWS
    quarter = flip(n, 2) * ((w // 8) % 2) + n * (1 - (w // 8) % 2)
    core = (w, flip(n, 1))
    zside = (w, flip(n, 2))
    cross = (w, flip(flip(n, 1), 2))
    x1, x2, x3 = (flip(w, 1), n), (flip(w, 2), n), (flip(flip(w, 1), 2), n)
    h1, h2 = (flip(w, 4), n), (flip(w, 8), flip(n, 2))

    loads = [
        pltpu.make_async_copy(a, b, load.at[i])
        for i, (a, b) in enumerate(
            (
                (order_h, order),
                (basis_h, basis),
                (sources_h, sources),
                (transfer_h, transfer),
                (cols_h, cols),
                (blocks_h, blocks),
                (out_basis_h, out_basis),
            )
        )
    ]
    for one in loads[:2]:
        one.start()
    barrier = pltpu.get_barrier_semaphore()
    partners = (core, zside, cross, x1, x2, x3, h1, h2)
    for who in partners:
        pl.semaphore_signal(barrier, inc=1, device_id=who, device_id_type=MESH)

    def remote(src, dst, i, j, who):
        return pltpu.make_async_remote_copy(
            src_ref=src, dst_ref=dst, send_sem=send.at[i], recv_sem=recv.at[j],
            device_id=who, device_id_type=MESH,
        )

    loads[0].wait()
    loads[2].start()
    turned = order[...].T
    for k in range(BLOCKS_DEV):
        order_col[k] = jnp.broadcast_to(turned[:, k : k + 1], (BLOCK, BLOCK))
    loads[1].wait()
    for one in loads[3:]:
        one.start()

    def move(b, _):
        at = pl.multiple_of(b * SCATTER_ROWS, SCATTER_ROWS)
        ids = lax.broadcasted_iota(I32, (SCATTER_ROWS, BLOCK), 0) + (first_row + at)
        hot = jnp.concatenate(
            [jnp.where(ids == order[k : k + 1, :], 1.0, 0.0).astype(BF16) for k in range(BLOCKS_DEV)],
            axis=1,
        )
        moved[pl.ds(at, SCATTER_ROWS), :] = dot(hot, basis[...]).astype(BF16)
        return 0

    lax.fori_loop(0, ROWS // SCATTER_ROWS, move, 0)
    loads[3].wait()
    pl.semaphore_wait(barrier, len(partners))
    side = n % 2
    send_tx = remote(transfer.at[0, side], transfer_x.at[side], 0, 0, x2)
    send_tx.start()

    loads[2].wait()
    half = quarter // 2
    q1, q2 = flip(quarter, 1), flip(quarter, 2)
    q3 = flip(q1, 2)

    def half_term(which):
        columns = sources[:, pl.ds(pl.multiple_of(which * HALF, HALF), HALF)]
        return lax.dot_general(
            columns, moved[...], (((0,), (0,)), ((), ())), preferred_element_type=F32
        )

    pair = (2, QUARTER, RANK)
    part_b[pl.ds(2 - 2 * half, 2)] = half_term(1 - half).astype(BF16).reshape(pair)
    send_c = [
        [
            remote(part_b.at[k, piece(p)], part_in.at[i, piece(p)], 2, 4 + p, who)
            for i, (k, who) in enumerate(((q2, zside), (q3, cross), (q1, core)))
        ]
        for p in range(PIECES)
    ]
    for p in range(PIECES):
        for one in send_c[p][:2]:
            one.start()
    term = half_term(half).reshape(pair)
    part[...] = term
    part_b[pl.ds(2 * half, 2)] = term.astype(BF16)
    for p in range(PIECES):
        send_c[p][2].start()

    def gather(k0, count):
        lanes = lax.broadcasted_iota(I32, (BLOCK, BLOCK), 1) + first_row
        rows = []
        for k in range(count):
            ids = order_col[k0 + k]
            rows.append(
                jnp.concatenate(
                    [jnp.where(lanes + c * BLOCK == ids, 1.0, 0.0).astype(BF16) for c in range(BLOCKS_DEV)],
                    axis=1,
                )
            )
        hot = jnp.concatenate(rows, axis=0)
        at = pl.multiple_of(k0 * BLOCK + HALO, BLOCK)
        permuted[pl.ds(at, count * BLOCK), :] = dot(hot, sources[...]).astype(BF16)

    first = (BLOCKS_DEV - REACH) * (1 - n // 2)
    gather(first, REACH)

    def halo_copy(up):
        if up:
            src, dst, who = permuted.at[pl.ds(ROWS, HALO)], permuted.at[pl.ds(0, HALO)], (n + 1) % 4
        else:
            src, dst, who = permuted.at[pl.ds(HALO, HALO)], permuted.at[pl.ds(ROWS + HALO, HALO)], (n + 3) % 4
        return pltpu.make_async_remote_copy(
            src_ref=src, dst_ref=dst, send_sem=halo_send.at[up], recv_sem=halo_recv.at[up],
            device_id=(w, who), device_id_type=MESH,
        )

    @pl.when(n < 2)
    def _():
        halo_copy(1).start()

    @pl.when(n >= 2)
    def _():
        halo_copy(0).start()

    loads[4].wait()
    listed = cols[...]
    lane = lax.broadcasted_iota(I32, (NEAR, BLOCKS_DEV), 1)
    entry = lax.broadcasted_iota(I32, (NEAR, BLOCKS_DEV), 0)
    rank = jnp.zeros((NEAR, BLOCKS_DEV), I32)
    for e in range(NEAR - 1):
        same = jnp.where(listed == listed[e : e + 1, :], 1, 0)
        rank = rank + jnp.where(entry > e, same, 0)
    slot = listed - lane - (w * 4 + n) * BLOCKS_DEV + REACH
    slot = slot + jnp.where(listed == w * CLUSTER_BLOCKS, -rank, rank)
    for d in range(OFFSETS):
        table_v[d : d + 1, :BLOCKS_DEV] = jnp.sum(
            jnp.where(slot == d, entry + 1, 0), axis=0, keepdims=True
        )
    table_copy = pltpu.make_async_copy(table_v, table_s, table_sem)
    table_copy.start()

    gather(BLOCKS_DEV - REACH - first, REACH)

    @pl.when(n == 2)
    def _():
        halo_copy(1).start()

    @pl.when(n == 1)
    def _():
        halo_copy(0).start()

    send_x = []
    for p in range(PIECES):
        remote(part_in.at[:, piece(p)], part_in.at[:, piece(p)], 2, 4 + p, core).wait_recv()
        own = part[quarter % 2, piece(p), :]
        for i in range(3):
            own = own + part_in[i, piece(p), :].astype(F32)
        c0[piece(p), :] = own.astype(BF16)
        send_x.append(
            [
                remote(c0.at[piece(p)], x_in.at[i, piece(p)], 3, 4 + PIECES + p, who)
                for i, who in ((1, x2), (0, x1), (2, x3))
            ]
        )
        for one in send_x[p]:
            one.start()
        if p < PIECES - 1:
            gather(REACH + p, 1)

    @pl.when(n == 0)
    def _():
        for k in range(REACH):
            permuted[k * BLOCK : (k + 1) * BLOCK, :] = permuted[HALO : HALO + BLOCK, :]

    @pl.when(n == 3)
    def _():
        for k in range(REACH):
            at = ROWS + HALO + k * BLOCK
            permuted[at : at + BLOCK, :] = permuted[ROWS + HALO - BLOCK : ROWS + HALO, :]

    send_tx.wait_recv()
    pass_tx = remote(transfer_x.at[side], transfer_x.at[side], 1, 1, core)
    pass_tx.start()
    gather(2 * REACH - 1, 1)
    gather(2 * REACH, REACH)
    table_copy.wait()
    loads[5].wait()

    def near_pair(p, _):
        def row(r):
            found = []
            for d in range(OFFSETS):
                at = table_s[d, r]
                block = blocks[r, jnp.maximum(at - 1, 0)]
                found.append(jnp.where(at > 0, block, jnp.zeros_like(block)))
            return found

        none = jnp.zeros((BLOCK, BLOCK), BF16)
        upper = jnp.concatenate(row(2 * p) + [none], axis=1)
        lower = jnp.concatenate([none] + row(2 * p + 1), axis=1)
        at = pl.multiple_of(p * 2 * BLOCK, 2 * BLOCK)
        found = dot(
            jnp.concatenate([upper, lower], axis=0),
            permuted[pl.ds(at, (OFFSETS + 1) * BLOCK), :],
        )
        near_o[0, pl.ds(at, 2 * BLOCK), :] = found[:, :HALF]
        near_o[1, pl.ds(at, 2 * BLOCK), :] = found[:, HALF:]
        return 0

    remote(transfer_x.at[1 - side], transfer_x.at[1 - side], 1, 1, core).wait_recv()
    send_h1 = []
    for p in range(PIECES):
        remote(x_in.at[:, piece(p)], x_in.at[:, piece(p)], 3, 4 + PIECES + p, x1).wait_recv()
        c1 = level(c0[piece(p), :], x_in[0, piece(p), :], transfer[0])
        c1x = level(x_in[1, piece(p), :], x_in[2, piece(p), :], transfer_x[...])
        c2[piece(p), :] = level(c1, c1x, transfer[1])
        send_h1.append(remote(c2.at[piece(p)], h1_in.at[piece(p)], 4, 4 + 2 * PIECES + p, h1))
        send_h1[p].start()

    lax.fori_loop(2, 6, near_pair, 0)

    send_h2 = []
    for p in range(PIECES):
        send_h1[p].wait_recv()
        c3[piece(p), :] = level(c2[piece(p), :], h1_in[piece(p), :], transfer[2])
        send_h2.append(remote(c3.at[piece(p)], h2_in.at[piece(p)], 5, 4 + 3 * PIECES + p, h2))
        send_h2[p].start()

    @pl.when(n > 0)
    def _():
        halo_copy(1).wait_recv()

    @pl.when(n < 3)
    def _():
        halo_copy(0).wait_recv()

    lax.fori_loop(0, 2, near_pair, 0)
    lax.fori_loop(6, 8, near_pair, 0)
    loads[6].wait()

    def share(i, k, p, who):
        return remote(coarse.at[k, piece(p)], coarse.at[k, piece(p)], 6, 2 + i // 2, who)

    send_q = []
    for p in range(PIECES):
        send_h2[p].wait_recv()
        coarse[quarter, piece(p), :] = level(c3[piece(p), :], h2_in[piece(p), :], transfer[3])
        send_q += [share(i, quarter, p, who) for i, who in enumerate((zside, cross, core))]
        for one in send_q[-3:]:
            one.start()
    remote(coarse.at[q1], coarse.at[q1], 6, 3, core).wait_recv()

    held = coarse[pl.ds(2 * half, 2)].reshape(HALF, RANK)

    def far_rows(b, _):
        at = pl.ds(pl.multiple_of(b * OUT_ROWS, OUT_ROWS), OUT_ROWS)
        own_o[at, :] = (dot_t(out_basis[at, :], held) + near_o[half, at, :]).astype(BF16)
        return 0

    lax.fori_loop(0, ROWS // OUT_ROWS, far_rows, 0)

    send_tx.wait_send()
    pass_tx.wait_send()
    remote(part_in, part_in, 2, 4, core).wait_send()
    remote(x_in, x_in, 3, 4, x1).wait_send()
    remote(c2, h1_in, 4, 4, h1).wait_send()
    remote(c3, h2_in, 5, 4, h2).wait_send()
    remote(part_in, part_in, 6, 4, core).wait_send()

    @pl.when(n < 3)
    def _():
        halo_copy(1).wait_send()

    @pl.when(n > 0)
    def _():
        halo_copy(0).wait_send()

    far_half = coarse.at[pl.ds(2 - 2 * half, 2)]
    remote(far_half, far_half, 6, 2, zside).wait_recv()
    other_o[...] = coarse[pl.ds(2 - 2 * half, 2)].reshape(HALF, RANK)


def tree(order, cols, sources, basis, blocks, transfer, out_basis):
    quarter = (QUARTER, RANK)
    scratch = [
        VMEM((BLOCKS_DEV, BLOCK), I32),
        VMEM((NEAR, BLOCKS_DEV), I32),
        VMEM((ROWS, RHS), BF16),
        VMEM((ROWS, RANK), BF16),
        VMEM((BLOCKS_DEV, NEAR, BLOCK, BLOCK), BF16),
        VMEM((4, 2, RANK, RANK), BF16),
        VMEM((BLOCKS_DEV, BLOCK, BLOCK), I32),
        VMEM((16, 128), I32),
        SMEM((16, 128), I32),
        VMEM((ROWS, RANK), BF16),
        VMEM((ROWS + 2 * HALO, RHS), BF16),
        VMEM((2, *quarter), F32),
        VMEM((4, *quarter), BF16),
        VMEM((3, *quarter), BF16),
        VMEM(quarter, BF16),
        VMEM((3, *quarter), BF16),
        VMEM((2, RANK, RANK), BF16),
        VMEM(quarter, BF16),
        VMEM(quarter, BF16),
        VMEM(quarter, BF16),
        VMEM(quarter, BF16),
        VMEM((4, *quarter), BF16),
        DMA((7,)),
        DMA,
        DMA((7,)),
        DMA((4 + 4 * PIECES,)),
        DMA((2,)),
        DMA((2,)),
    ]
    return pl.pallas_call(
        tree_kernel,
        out_shape=(
            VMEM((HALF, RANK), BF16),
            VMEM((2, ROWS, HALF), F32),
            VMEM((ROWS, HALF), BF16),
            VMEM((ROWS, RANK), BF16),
        ),
        in_specs=[pl.BlockSpec(memory_space=pltpu.HBM)] * 7,
        out_specs=[pl.BlockSpec(memory_space=VMEM)] * 4,
        scratch_shapes=scratch,
        compiler_params=pltpu.CompilerParams(
            collective_id=0, has_side_effects=True, vmem_limit_bytes=44 << 20
        ),
        name="tree",
    )(order, cols, sources, basis, blocks, transfer, out_basis)


def far_kernel(basis, other, near, own, out_h, out, own_sem, store):
    count = ROWS // LAST_ROWS
    w, n = lax.axis_index("wide"), lax.axis_index("narrow")
    half = (flip(n, 2) * ((w // 8) % 2) + n * (1 - (w // 8) % 2)) // 2

    def columns(which):
        return pl.ds(pl.multiple_of(which * HALF, HALF), HALF)

    send_own = pltpu.make_async_copy(own, out_h.at[:, columns(half)], own_sem)
    send_own.start()
    stores = []
    for i in range(count):
        at = pl.ds(i * LAST_ROWS, LAST_ROWS)
        out[at, :] = (dot_t(basis[at, :], other[...]) + near[1 - half, at, :]).astype(BF16)
        stores.append(
            pltpu.make_async_copy(out.at[at], out_h.at[at, columns(1 - half)], store.at[i])
        )
        stores[-1].start()
    for one in stores:
        one.wait()
    send_own.wait()


def far(basis, other, near, own):
    return pl.pallas_call(
        far_kernel,
        out_shape=jax.ShapeDtypeStruct((ROWS, RHS), BF16),
        in_specs=[pl.BlockSpec(memory_space=VMEM)] * 4,
        out_specs=pl.BlockSpec(memory_space=pl.ANY),
        scratch_shapes=[VMEM((ROWS, HALF), BF16), DMA, DMA((ROWS // LAST_ROWS,))],
        compiler_params=pltpu.CompilerParams(vmem_limit_bytes=6 << 20),
        name="far",
    )(basis, other, near, own)


def on_device(sources, order, near_cols, near_blocks, in_basis, transfer, out_basis):
    given = (
        order.reshape(BLOCKS_DEV, BLOCK), near_cols.T, sources, in_basis, near_blocks, transfer[:, 0],
        out_basis,
    )
    other, near, own, basis = tree(*(pltpu.with_memory_space_constraint(x, pltpu.HBM) for x in given))
    return far(basis, other, near, own)


def solution(mesh):
    return jax.shard_map(
        on_device,
        mesh=mesh,
        in_specs=(
            P(("wide", "narrow"), None),
            P(("wide", "narrow")),
            P(("wide", "narrow"), None),
            P(("wide", "narrow"), None, None, None),
            P(("wide", "narrow"), None),
            P(None, "wide", None, None, None),
            P(("wide", "narrow"), None),
        ),
        out_specs=P(("wide", "narrow"), None),
        check_vma=False,
    )
```
